256 devices in a mesh: fsdp: 32 (over x, z_lo, core), tp: 8 (over z_hi, y).
Axes of the slice: x: 4, y: 4, z: 8 (z_hi: 2, z_lo: 4; z = z_hi * 4 + z_lo), core: 2. Of those that a mesh axis runs over, the one named last changes fastest.
Arguments:
- grad_part: float32 [32, 4, 512, 8192], P('fsdp', None, None, 'tp'), may hold values from -6 to 6
- block_of_slot: int32 [64], replicated, may hold values from 0 to 63, each once
- stat_left: float32 [64, 512, 512], P('fsdp', 'tp'), may hold values from -6 to 6
- stat_right: float32 [64, 512, 512], P('fsdp', 'tp'), may hold values from -6 to 6
- basis_left: float32 [64, 512, 512], P('fsdp', 'tp'), may hold values from -0.25 to 0.25
- basis_right: float32 [64, 512, 512], P('fsdp', 'tp'), may hold values from -0.25 to 0.25
- moment: float32 [64, 512, 512], P('fsdp', 'tp'), may hold values from -4 to 4
- second: float32 [64, 512, 512], P('fsdp', 'tp'), may hold values from 0.05 to 2
Outputs:
- update: bfloat16 [4, 512, 8192], P(None, 'fsdp', 'tp')
- new_left: float32 [64, 512, 512], P('fsdp', 'tp')
- new_right: float32 [64, 512, 512], P('fsdp', 'tp')
- new_moment: float32 [64, 512, 512], P('fsdp', 'tp')
- new_second: float32 [64, 512, 512], P('fsdp', 'tp')
The draws below stay inside these ranges and needn't reach their ends.
Inputs may be any that keep to these rules, and one draw needn't show every extreme that they name: Slot s, held by fsdp index s // 2, carries the state of block block_of_slot[s]; every block has exactly one slot.
All inputs are finite; a program needn't handle non-finite values.
Results may differ from the reference program's by a relative error of at most 0.001.
Values may be sent and summed in bfloat16 or wider, within the bound.
A program may use at most 128 MiB of HBM per device.

```python
import math
import jax
import jax.numpy as jnp
from jax import lax

D = 8192
BS = 512
SL = 64
CB = 16
NB = 64
PAN = 4
N_FSDP = 32
N_TP = 8


def strengthened(result, key, source, target, blocks, factor):
    owner, partner = [(jnp.arange(result.shape[dim]) // (result.shape[dim] // blocks)).reshape([-1 if axis == dim else 1 for axis in range(result.ndim)]) for dim in (source, target)]
    chosen = jax.random.permutation(key, blocks)[partner]
    strong = (owner == chosen) | (owner == (partner + blocks // 2) % blocks)
    return jnp.where(strong, factor * result, result)


def level_of(stream_key, extent, pieces, low, largest):
    level, own = 1.0, jax.random.fold_in(stream_key, 6)
    for axis_at, parts in pieces:
        heights = jnp.exp(jax.random.uniform(jax.random.fold_in(own, axis_at), (parts,), jnp.float32, low / len(pieces), largest / len(pieces)))
        level = level * jnp.repeat(heights, extent[axis_at] // parts).reshape([-1 if axis == axis_at else 1 for axis in range(len(extent))])
    return level


def gaussian(key, extent, deviation, reach, pieces=(), dtype=jnp.bfloat16):
    values = deviation * jax.random.normal(key, extent, jnp.float32)
    if pieces:
        values = values * level_of(key, extent, pieces, -0.22, 0.18)
    return jnp.clip(values, -reach, reach).astype(dtype)


def heavy_noise(key, extent, scale, bound, cuts, heavy, kind=jnp.bfloat16):
    drawn = scale * jax.random.normal(key, extent, jnp.float32)
    if cuts:
        drawn = drawn * level_of(key, extent, cuts, -0.22, 0.18)
    return jnp.clip(strengthened(drawn, jax.random.fold_in(key, 3), *heavy), -bound, bound).astype(kind)


def setup_inputs(seed: int = 0) -> dict:
    splits = jax.random.split(jax.random.key(seed), 9)
    return {
        "grad_part": heavy_noise(splits[0], (N_FSDP, PAN, BS, D), 0.2, 6.0, ((0, 32), (3, 8)), (0, 2, 32, 2.75), jnp.float32),
        "block_of_slot": jax.random.permutation(splits[1], NB).astype(jnp.int32),
        "stat_left": gaussian(splits[2], (NB, BS, BS), 1.0, 6.0, ((0, 32), (1, 8)), jnp.float32),
        "stat_right": gaussian(splits[3], (NB, BS, BS), 1.0, 6.0, ((0, 32), (1, 8)), jnp.float32),
        "basis_left": gaussian(splits[4], (NB, BS, BS), BS ** -0.5, 0.25, ((0, 32), (1, 8)), jnp.float32),
        "basis_right": gaussian(splits[5], (NB, BS, BS), BS ** -0.5, 0.25, ((0, 32), (1, 8)), jnp.float32),
        "moment": gaussian(splits[6], (NB, BS, BS), 0.5, 4.0, ((0, 32), (1, 8)), jnp.float32),
        "second": jnp.clip(jnp.exp(math.log(2.0) - 3.6888794 * jax.random.uniform(splits[7], (NB, BS, BS), jnp.float32) ** level_of(splits[7], (NB, BS, BS), ((0, 32), (1, 8)), -0.2, 0.2)), 0.05, 2.0),
    }


first_decay = 0.9
second_decay = 0.95
epsilon = 1e-08
highest = lax.Precision.HIGHEST

def product(form, left, right):
    return jnp.einsum(form, left.astype(jnp.float32), right.astype(jnp.float32), precision=highest)

def reference(grad_part, block_of_slot, stat_left, stat_right, basis_left, basis_right, moment, second):
    grad = lax.optimization_barrier(jnp.sum(grad_part, axis=0))
    blocks = jnp.transpose(grad.reshape(PAN, BS, N_TP, CB, SL), (0, 3, 2, 4, 1)).reshape(NB, BS, BS)
    slot_grad = jnp.take(blocks, block_of_slot.astype(jnp.int32), axis=0)
    new_left = second_decay * stat_left + (1.0 - second_decay) * product('bki,bkj->bij', slot_grad, slot_grad)
    new_right = second_decay * stat_right + (1.0 - second_decay) * product('bik,bjk->bij', slot_grad, slot_grad)
    partial_rot = product('bik,bkj->bij', basis_right, slot_grad)
    rotated = product('bir,bmr->bim', partial_rot, basis_left)
    new_moment = first_decay * moment + (1.0 - first_decay) * rotated
    new_second = second_decay * second + (1.0 - second_decay) * rotated * rotated
    direction = new_moment / (jnp.sqrt(new_second) + epsilon)
    half_back = product('bkr,brm->bkm', direction, basis_left)
    back = product('bki,bkm->bim', basis_right, half_back).astype(jnp.bfloat16)
    ordered = jnp.zeros((NB, BS, BS), jnp.bfloat16).at[block_of_slot.astype(jnp.int32)].set(back)
    update = jnp.transpose(ordered.reshape(PAN, CB, N_TP, SL, BS), (0, 4, 2, 1, 3)).reshape(PAN, BS, D)
    return (update, new_left, new_right, new_moment, new_second)
```

```python
import jax
import jax.numpy as jnp
from jax import lax
from jax.experimental import pallas as pl
from jax.experimental.pallas import tpu as pltpu
from jax.sharding import PartitionSpec as P

first_decay = 0.9
second_decay = 0.95
epsilon = 1e-08
MESH = pl.DeviceIdType.MESH
f32, bf16, i16, i32 = jnp.float32, jnp.bfloat16, jnp.int16, jnp.int32
FAR = (2, 1, 3)


def roll_half(v):
    return pltpu.roll(v, 64, 1)


def lane_iota(rows):
    return lax.broadcasted_iota(i32, (rows, 128), 1)


def split(v):
    high = v.astype(bf16)
    return high, (v - high.astype(f32)).astype(bf16)


def dot(a, b, dims):
    return lax.dot_general(a, b, (dims, ((), ())), preferred_element_type=f32)


PLAIN = ((1,), (0,))
MINOR = ((1,), (1,))


def dot3(a, bh, bl, dims):
    ah, al = split(a)
    return dot(ah, bh, dims) + (dot(ah, bl, dims) + dot(al, bh, dims))


def encode(v, ref):
    top = jnp.max(jnp.abs(v), axis=0, keepdims=True)
    power = jnp.ceil(jnp.log2(jnp.maximum(top, 1e-30) * (1.0 / 32500.0)))
    ref[pl.ds(0, 256), :] = jnp.round(v * jnp.exp2(-power)).astype(i32).astype(i16)
    ref[pl.ds(256, 16), :] = jnp.broadcast_to(power, (16, 128)).astype(i32).astype(i16)


def scale_of(ref):
    return jnp.exp2(ref[pl.ds(256, 16), :].astype(i32).astype(f32))[0:1]


def decode(ref):
    return ref[pl.ds(0, 256), :].astype(i32).astype(f32) * scale_of(ref)


def kernel(
    bos, inv, grad_h, sl_h, sr_h, bl_h, br_h, mo_h, se_h,
    upd_h, nl_h, nr_h, nm_h, ns_h,
    g, sl, sr, bl, br, mo, se, upd,
    cs, cr, xs, xr, zs, zr, za, gslab, ag, ah, left, rmsg, rc, rct, gt, hb, tmp, bk, a2s, a2r,
    loc, g_sem, out_sem, c_s, c_r, x_s, x_r, z_s, z_r, l_s, l_r, r_s, r_r, g_s, g_r, h_s, h_r, a_s, a_r,
):
    f = lax.axis_index("fsdp")
    t = lax.axis_index("tp")
    x, zl, c = f // 8, (f // 2) % 4, f % 2
    zh, y = t // 4, t % 4

    def fdev(x_, z_, c_):
        return ((x_ * 4 + z_) * 2 + c_, t)

    def tdev(zh_, y_):
        return (f, zh_ * 4 + y_)

    def remote(src, dst, ss, rs, dev):
        return pltpu.make_async_remote_copy(
            src_ref=src, dst_ref=dst, send_sem=ss, recv_sem=rs, device_id=dev, device_id_type=MESH
        )

    loads = [
        pltpu.make_async_copy(src, dst, loc.at[i])
        for i, (src, dst) in enumerate(((bl_h, bl), (br_h, br), (sl_h, sl), (sr_h, sr), (mo_h, mo), (se_h, se)))
    ]

    def grad_load(i):
        p, u = i // 8, i % 8
        return pltpu.make_async_copy(
            grad_h.at[p, :, :, pl.ds(pl.multiple_of(u * 128, 128), 128)], g.at[pl.ds(2 * i, 2)], g_sem.at[i]
        )

    loads[0].start()
    loads[1].start()

    @pl.loop(0, 32)
    def _(i):
        grad_load(i).start()

    for cp in loads[2:]:
        cp.start()

    barrier = pltpu.get_barrier_semaphore()

    @pl.loop(1, 32)
    def _(d):
        pl.semaphore_signal(barrier, inc=1, device_id=((f + d) % 32, t), device_id_type=MESH)

    @pl.loop(1, 8)
    def _(d):
        pl.semaphore_signal(barrier, inc=1, device_id=(f, (t + d) % 8), device_id_type=MESH)

    def core_copy(s, dx):
        return remote(cs.at[s, dx], cr.at[s, dx], c_s.at[s, dx], c_r.at[s, dx], fdev(x, zl, 1 - c))

    def x_copy(s, dx, z):
        return remote(
            xs.at[s, dx - 1, z], xr.at[s, dx - 1, z], x_s.at[s, dx - 1, z], x_r.at[s, dx - 1, z],
            fdev((x + dx) % 4, zl, c),
        )

    def z_copy(s, dz):
        return remote(
            zs.at[s, dz - 1], zr.at[s, dz - 1], z_s.at[s, dz - 1], z_r.at[s, dz - 1],
            fdev(x, (zl + dz) % 4, c),
        )

    def tp_copies(view, ss, rs):
        own = view(t)
        other = view((1 - zh) * 4 + y)
        first = [remote(own, own, ss(0), rs(0), tdev(1 - zh, y))]
        first += [remote(own, own, ss(d), rs(d), tdev(zh, (y + d) % 4)) for d in FAR]
        second = [remote(other, other, ss(3 + d), rs(3 + d), tdev(zh, (y + d) % 4)) for d in FAR]
        return first, second

    left_first, left_second = tp_copies(
        lambda k: left.at[:, :, pl.ds(pl.multiple_of(k * 64, 64), 64), :],
        lambda i: l_s.at[i], lambda i: l_r.at[i],
    )
    g_copies = [
        tp_copies(lambda k, s=s: ag.at[s, k], lambda i, s=s: g_s.at[s, i], lambda i, s=s: g_r.at[s, i])
        for s in range(2)
    ]
    h_copies = [
        tp_copies(lambda k, s=s: ah.at[s, k], lambda i, s=s: h_s.at[s, i], lambda i, s=s: h_r.at[s, i])
        for s in range(2)
    ]

    def right_copy(d):
        k = (t + d) % 8
        rows = rc.at[:, pl.ds(pl.multiple_of(t * 64, 64), 64), :]
        return remote(rmsg.at[k], rows, r_s.at[d], r_r.at[d], (f, k))

    def a2a_copy(d):
        k = (f + d) % 32
        return remote(a2s.at[k], a2r.at[f], a_s.at[d], a_r.at[d], (k, t))

    def start(copies):
        for cp in copies:
            cp.start()

    loads[0].wait()
    own_rows = pl.ds(pl.multiple_of(t * 64, 64), 64)
    for s in range(2):
        high, low = split(bl[s])
        left[s, 0, own_rows, :] = high
        left[s, 1, own_rows, :] = low
    loads[1].wait()
    lanes = lane_iota(64)
    for u in range(4):
        a = br[0, :, u * 128 : u * 128 + 128]
        b = br[1, :, u * 128 : u * 128 + 128]
        for k, v in ((2 * u, jnp.where(lanes < 64, a, roll_half(b))), (2 * u + 1, jnp.where(lanes < 64, roll_half(a), b))):
            high, low = split(v)
            rmsg[k, 0] = high
            rmsg[k, 1] = low
    rc[:, own_rows, :] = rmsg[t]

    pl.semaphore_wait(barrier, 38)
    start(left_first)

    @pl.loop(1, 8)
    def _(d):
        right_copy(d).start()

    def extract(slot):
        b = bos[slot]
        half = b % 2
        pair = b // 2
        near = g[pair * 2 + half]
        away = g[pair * 2 + 1 - half]
        upper = (lane_iota(256) >= 64).astype(i32)
        return jnp.where(upper == half, near, roll_half(away))

    def slot_of(s, dx, z, core):
        return ((((x + dx) % 4) * 4 + z) * 2 + core) * 2 + s

    def core_stage(s):
        for dx in (2, 1, 3, 0):

            @pl.loop(0, 4)
            def _(z):
                cs[s, dx, z] = extract(slot_of(s, dx, z, 1 - c))

            core_copy(s, dx).start()

    def x_stage(s):
        for dx in FAR:
            core_copy(s, dx).wait_recv()

            @pl.loop(0, 4)
            def _(i):
                z = (zl + 1 + i) % 4
                encode(extract(slot_of(s, dx, z, c)) + cr[s, dx, z], xs.at[s, dx - 1, z])
                x_copy(s, dx, z).start()

    def x_sum(s, z):
        for dx in FAR:
            x_copy(s, dx, z).wait_recv()
        total = extract(slot_of(s, 0, z, c)) + cr[s, 0, z]
        for dx in FAR:
            total += decode(xr.at[s, dx - 1, z])
        return total

    def z_stage(s):
        core_copy(s, 0).wait_recv()

        @pl.loop(1, 4)
        def _(dz):
            encode(x_sum(s, (zl + dz) % 4), zs.at[s, dz - 1])
            z_copy(s, dz).start()

        za[s] = x_sum(s, zl)

    def g_stage(s):
        total = za[s]
        for dz in range(1, 4):
            z_copy(s, dz).wait_recv()
            total += decode(zr.at[s, dz - 1])
        turned = total.T
        a, b = turned[0:64], turned[64:128]
        gslab[s, :, 0:256] = a
        gslab[s, :, 256:512] = b
        encode(jnp.concatenate([a[:, :128], a[:, 128:], b[:, :128], b[:, 128:]], axis=0), ag.at[s, t])
        start(g_copies[s][0])

    def forward(copies):
        copies[0][0].wait_recv()
        start(copies[1])

    def gathered(copies, messages, s, store):
        for cp in copies[0][1:] + copies[1]:
            cp.wait_recv()

        @pl.loop(0, 8)
        def _(k):
            v = decode(messages.at[s, k])
            rows = pl.ds(pl.multiple_of(k * 64, 64), 64)
            for q in range(4):
                high, low = split(v[q * 64 : q * 64 + 64])
                store[s, 0, rows, q * 128 : q * 128 + 128] = high
                store[s, 1, rows, q * 128 : q * 128 + 128] = low

    def put(ref, dst, i, s):
        return pltpu.make_async_copy(ref.at[s], dst.at[s], out_sem.at[i, s])

    def rotate(s):
        gathered(g_copies[s], ag, s, gt)
        partial = dot3(br[s], gt[s, 0], gt[s, 1], PLAIN)
        rotated = dot3(partial, left[s, 0], left[s, 1], MINOR)
        new_moment = first_decay * mo[s] + (1.0 - first_decay) * rotated
        new_second = second_decay * se[s] + (1.0 - second_decay) * rotated * rotated
        mo[s] = new_moment
        se[s] = new_second
        direction = new_moment / (jnp.sqrt(new_second) + epsilon)
        half = dot3(direction, left[s, 0], left[s, 1], PLAIN)
        encode(jnp.concatenate([half[:, q * 128 : q * 128 + 128] for q in range(4)], axis=0), ah.at[s, t])
        start(h_copies[s][0])
        put(mo, nm_h, 0, s).start()
        put(se, ns_h, 1, s).start()

    def statistics(s):
        right = dot3(gslab[s], gt[s, 0], gt[s, 1], MINOR)
        sr[s] = second_decay * sr[s] + (1.0 - second_decay) * right
        put(sr, nr_h, 2, s).start()
        cols = pl.ds(pl.multiple_of((t // 2) * 128, 128), 128)
        rows = gt[s, 0, :, cols].astype(f32) + gt[s, 1, :, cols].astype(f32)
        tmp[...] = rows.T
        mine = tmp[pl.ds(pl.multiple_of((t % 2) * 64, 64), 64), :]
        out = dot3(mine, gt[s, 0], gt[s, 1], PLAIN)
        sl[s] = second_decay * sl[s] + (1.0 - second_decay) * out
        put(sl, nl_h, 3, s).start()

    def back(s):
        gathered(h_copies[s], ah, s, hb)
        bk[pl.ds(s * 64, 64), :] = dot3(rct[pl.ds(s * 64, 64), :], hb[s, 0], hb[s, 1], PLAIN)

    @pl.loop(0, 32)
    def _(i):
        grad_load(i).wait()

    core_stage(0)
    x_stage(0)
    core_stage(1)
    x_stage(1)
    forward((left_first, left_second))
    z_stage(0)
    for cp in loads[2:]:
        cp.wait()

    @pl.loop(1, 8)
    def _(d):
        right_copy(d).wait_recv()

    rct[...] = (rc[0].astype(f32) + rc[1].astype(f32)).T
    g_stage(0)
    z_stage(1)
    forward(g_copies[0])
    g_stage(1)
    for cp in left_first[1:] + left_second:
        cp.wait_recv()
    rotate(0)
    forward(g_copies[1])
    rotate(1)
    forward(h_copies[0])
    statistics(0)
    forward(h_copies[1])
    statistics(1)
    back(0)
    back(1)
    rows = bk[...].T.astype(bf16)
    for k in range(32):
        a2s[k] = rows[k * 16 : k * 16 + 16]
    a2r[f] = a2s[f]

    @pl.loop(1, 32)
    def _(d):
        a2a_copy(d).start()

    for s in range(2):
        for dx in range(4):
            core_copy(s, dx).wait_send()
        for dx in FAR:

            @pl.loop(0, 4)
            def _(z):
                x_copy(s, dx, z).wait_send()

        for dz in range(1, 4):
            z_copy(s, dz).wait_send()
        for cp in g_copies[s][0] + g_copies[s][1] + h_copies[s][0] + h_copies[s][1]:
            cp.wait_send()
        for i, (ref, dst) in enumerate(((mo, nm_h), (se, ns_h), (sr, nr_h), (sl, nl_h))):
            put(ref, dst, i, s).wait()
    for cp in left_first + left_second:
        cp.wait_send()

    @pl.loop(1, 8)
    def _(d):
        right_copy(d).wait_send()

    @pl.loop(1, 32)
    def _(d):
        a2a_copy(d).wait()

    low_lanes = lane_iota(16) < 64

    @pl.loop(0, 4)
    def _(p):
        for u in range(8):
            first, second = inv[p * 16 + 2 * u], inv[p * 16 + 2 * u + 1]
            a = a2r[first // 2].astype(f32)
            b = a2r[second // 2].astype(f32)
            a = jnp.where((lane_iota(16) * 0 + first % 2) == 0, a, roll_half(a))
            b = jnp.where((lane_iota(16) * 0 + second % 2) == 1, b, roll_half(b))
            upd[p, :, u * 128 : u * 128 + 128] = jnp.where(low_lanes, a, b).astype(bf16)

    cp = pltpu.make_async_copy(upd, upd_h, loc.at[6])
    cp.start()
    cp.wait()


def local(grad_part, block_of_slot, stat_left, stat_right, basis_left, basis_right, moment, second):
    order = jnp.arange(64, dtype=i32)
    inverse = jnp.sum(jnp.where(block_of_slot[None, :] == order[:, None], order[None, :], 0), axis=1)
    smem = pl.BlockSpec(memory_space=pltpu.SMEM)
    hbm = pl.BlockSpec(memory_space=pl.ANY)
    state = jax.ShapeDtypeStruct((2, 64, 512), f32)
    v = pltpu.VMEM
    dma = pltpu.SemaphoreType.DMA
    return pl.pallas_call(
        kernel,
        name="step",
        out_shape=(jax.ShapeDtypeStruct((4, 16, 1024), bf16), state, state, state, state),
        in_specs=[smem, smem] + [hbm] * 7,
        out_specs=(hbm,) * 5,
        scratch_shapes=[
            v((64, 256, 128), f32),
            *[v((2, 64, 512), f32)] * 6,
            v((4, 16, 1024), bf16),
            v((2, 4, 4, 256, 128), f32),
            v((2, 4, 4, 256, 128), f32),
            v((2, 3, 4, 272, 128), i16),
            v((2, 3, 4, 272, 128), i16),
            v((2, 3, 272, 128), i16),
            v((2, 3, 272, 128), i16),
            v((2, 256, 128), f32),
            v((2, 64, 512), f32),
            v((2, 8, 272, 128), i16),
            v((2, 8, 272, 128), i16),
            v((2, 2, 512, 512), bf16),
            v((8, 2, 64, 128), bf16),
            v((2, 512, 128), bf16),
            v((128, 512), f32),
            v((2, 2, 512, 512), bf16),
            v((2, 2, 512, 512), bf16),
            v((128, 512), f32),
            v((128, 512), f32),
            v((32, 16, 128), bf16),
            v((32, 16, 128), bf16),
            dma((8,)),
            dma((32,)),
            dma((4, 2)),
            *[dma((2, 4))] * 2,
            *[dma((2, 3, 4))] * 2,
            *[dma((2, 3))] * 2,
            *[dma((7,))] * 2,
            *[dma((8,))] * 2,
            *[dma((2, 7))] * 4,
            *[dma((32,))] * 2,
        ],
        compiler_params=pltpu.CompilerParams(
            collective_id=0, has_side_effects=True, vmem_limit_bytes=52 * 2**20
        ),
    )(block_of_slot, inverse, grad_part.reshape(4, 2, 256, 1024), stat_left, stat_right, basis_left, basis_right, moment, second)


def solution(mesh):
    return jax.shard_map(
        local,
        mesh=mesh,
        in_specs=(
            P("fsdp", None, None, "tp"),
            P(),
            P("fsdp", "tp", None),
            P("fsdp", "tp", None),
            P("fsdp", "tp", None),
            P("fsdp", "tp", None),
            P("fsdp", "tp", None),
            P("fsdp", "tp", None),
        ),
        out_specs=(
            P(None, "fsdp", "tp"),
            P("fsdp", "tp", None),
            P("fsdp", "tp", None),
            P("fsdp", "tp", None),
            P("fsdp", "tp", None),
        ),
        check_vma=False,
    )
```

```python
import jax
import jax.numpy as jnp
from jax import lax
from jax.experimental import pallas as pl
from jax.experimental.pallas import tpu as pltpu
from jax.sharding import PartitionSpec as P

first_decay = 0.9
second_decay = 0.95
epsilon = 1e-08
MESH = pl.DeviceIdType.MESH
f32, bf16, i16, i32 = jnp.float32, jnp.bfloat16, jnp.int16, jnp.int32
FAR = (2, 1, 3)
vmem_bytes = 64 * 2**20 - 19 * 2**16


def roll_half(v):
    return pltpu.roll(v, 64, 1)


def lane_iota(rows):
    return lax.broadcasted_iota(i32, (rows, 128), 1)


def split(v):
    high = v.astype(bf16)
    return high, (v - high.astype(f32)).astype(bf16)


def dot(a, b, dims):
    return lax.dot_general(a, b, (dims, ((), ())), preferred_element_type=f32)


PLAIN = ((1,), (0,))
MINOR = ((1,), (1,))


def dot3(a, bh, bl, dims):
    ah, al = split(a)
    return dot(ah, bh, dims) + (dot(ah, bl, dims) + dot(al, bh, dims))


def encode(v, ref):
    top = jnp.max(jnp.abs(v), axis=0, keepdims=True)
    power = jnp.ceil(jnp.log2(jnp.maximum(top, 1e-30) * (1.0 / 32500.0)))
    ref[pl.ds(0, 256), :] = jnp.round(v * jnp.exp2(-power)).astype(i32).astype(i16)
    ref[pl.ds(256, 16), :] = jnp.broadcast_to(power, (16, 128)).astype(i32).astype(i16)


def scale_of(ref):
    return jnp.exp2(ref[pl.ds(256, 16), :].astype(i32).astype(f32))[0:1]


def decode(ref):
    return ref[pl.ds(0, 256), :].astype(i32).astype(f32) * scale_of(ref)


def kernel(
    bos, grad_h, sl_h, sr_h, bl_h, br_h, mo_h, se_h,
    a2r, nl, nr, nm, ns,
    g, sl, sr, bl, br, mo, se,
    cs, cr, xq, xqr, xs, xr, zs, zr, za, gslab, ag, ah, lm, left, rmsg, rc, rct, gt, hb, tmp, bk, part, a2s,
    loc, g_sem, out_sem, c_s, c_r, q_s, q_r, x_s, x_r, z_s, z_r, l_s, l_r, r_s, r_r, g_s, g_r, h_s, h_r, a_s, a_r,
):
    f = lax.axis_index("fsdp")
    t = lax.axis_index("tp")
    x, zl, c = f // 8, (f // 2) % 4, f % 2
    zh, y = t // 4, t % 4

    def fdev(x_, z_, c_):
        return ((x_ * 4 + z_) * 2 + c_, t)

    def tdev(zh_, y_):
        return (f, zh_ * 4 + y_)

    def remote(src, dst, ss, rs, dev):
        return pltpu.make_async_remote_copy(
            src_ref=src, dst_ref=dst, send_sem=ss, recv_sem=rs, device_id=dev, device_id_type=MESH
        )

    loads = [
        pltpu.make_async_copy(src, dst, loc.at[i])
        for i, (src, dst) in enumerate(((bl_h, bl), (br_h, br), (sl_h, sl), (sr_h, sr), (mo_h, mo), (se_h, se)))
    ]

    def grad_load(i):
        return pltpu.make_async_copy(
            grad_h.at[:, :, pl.ds(pl.multiple_of(i * 128, 128), 128)], g.at[pl.ds(8 * i, 8)], g_sem.at[i]
        )

    @pl.loop(0, 8)
    def _(i):
        grad_load(i).start()

    for cp in loads:
        cp.start()

    barrier = pltpu.get_barrier_semaphore()

    @pl.loop(1, 32)
    def _(d):
        pl.semaphore_signal(barrier, inc=1, device_id=((f + d) % 32, t), device_id_type=MESH)

    @pl.loop(1, 8)
    def _(d):
        pl.semaphore_signal(barrier, inc=1, device_id=(f, (t + d) % 8), device_id_type=MESH)

    def core_copy(s, dx):
        return remote(cs.at[s, dx], cr.at[s, dx], c_s.at[s, dx], c_r.at[s, dx], fdev(x, zl, 1 - c))

    def relay_copy(s, i):
        return remote(
            xq.at[s, i], xqr.at[s, i], q_s.at[s, i], q_r.at[s, i], fdev((x + 1 + i // 2 * 2) % 4, zl, c)
        )

    def x_copy(s, way, i):
        return remote(
            xs.at[s, way, i], xr.at[s, way, i], x_s.at[s, way, i], x_r.at[s, way, i],
            fdev((x + 1 + 2 * way) % 4, zl, c),
        )

    def z_copy(s, dz):
        return remote(
            zs.at[s, dz - 1], zr.at[s, dz - 1], z_s.at[s, dz - 1], z_r.at[s, dz - 1],
            fdev(x, (zl + dz) % 4, c),
        )

    def tp_copies(view, ss, rs):
        own = view(t)
        other = view((1 - zh) * 4 + y)
        first = [remote(own, own, ss(0), rs(0), tdev(1 - zh, y))]
        first += [remote(own, own, ss(d), rs(d), tdev(zh, (y + d) % 4)) for d in FAR]
        second = [remote(other, other, ss(3 + d), rs(3 + d), tdev(zh, (y + d) % 4)) for d in FAR]
        return first, second

    left_first, left_second = tp_copies(lambda k: lm.at[k], lambda i: l_s.at[i], lambda i: l_r.at[i])
    g_copies = [
        tp_copies(lambda k, s=s: ag.at[s, k], lambda i, s=s: g_s.at[s, i], lambda i, s=s: g_r.at[s, i])
        for s in range(2)
    ]
    h_copies = [
        tp_copies(lambda k, s=s: ah.at[s, k], lambda i, s=s: h_s.at[s, i], lambda i, s=s: h_r.at[s, i])
        for s in range(2)
    ]

    def right_copy(d):
        k = (t + d) % 8
        return remote(rmsg.at[k], rc.at[t], r_s.at[d], r_r.at[d], (f, k))

    def a2a_copy(d):
        k = (f + d) % 32
        return remote(a2s.at[k], a2r.at[f], a_s.at[d], a_r.at[d], (k, t))

    def start(copies):
        for cp in copies:
            cp.start()

    leaving = {}

    def left_device(*name):
        leaving.pop(name)()

    def wait_sent(copies):
        for cp in copies:
            cp.wait_send()

    pl.semaphore_wait(barrier, 38)

    def stacked(v):
        return jnp.concatenate([v[:, q * 128 : q * 128 + 128] for q in range(4)], axis=0)

    def send_left():
        loads[0].wait()
        for s in range(2):
            encode(stacked(bl[s]), lm.at[t, s])
        start(left_first)
        leaving["left", 0] = lambda: wait_sent(left_first)

    def send_right():
        lanes = lane_iota(64)
        for u in range(4):
            a = br[0, :, u * 128 : u * 128 + 128]
            b = br[1, :, u * 128 : u * 128 + 128]
            even, odd = jnp.where(lanes < 64, a, roll_half(b)), jnp.where(lanes < 64, roll_half(a), b)
            for k, v in ((2 * u, even), (2 * u + 1, odd)):
                high, low = split(v)
                rmsg[k, 0] = high
                rmsg[k, 1] = low
        rc[t] = rmsg[t]

        @pl.loop(1, 8)
        def _(d):
            right_copy(d).start()

        def sent():
            @pl.loop(1, 8)
            def _(d):
                right_copy(d).wait_send()

        leaving["right",] = sent

    def extract(slot):
        b = bos[slot]
        half = b % 2
        first = ((b % 16) // 2 * 4 + b // 16) * 2
        near = g[first + half]
        away = g[first + 1 - half]
        upper = (lane_iota(256) >= 64).astype(i32)
        return jnp.where(upper == half, near, roll_half(away))

    def slot_of(s, dx, z, core):
        return ((((x + dx) % 4) * 4 + z) * 2 + core) * 2 + s

    def core_part(s, dx):
        @pl.loop(0, 4)
        def _(z):
            cs[s, dx, z] = extract(slot_of(s, dx, z, 1 - c))

        core_copy(s, dx).start()
        leaving["core", s, dx] = lambda: core_copy(s, dx).wait_send()

    def pair_sum(s, dx, z):
        return extract(slot_of(s, dx, z, c)) + cr[s, dx, z]

    def relay_stage(s):
        core_copy(s, 2).wait_recv()

        @pl.loop(0, 4)
        def _(j):
            i = j // 2 + 2 * (j % 2)
            encode(pair_sum(s, 2, (zl + 1 + i) % 4), xq.at[s, i])
            relay_copy(s, i).start()

        def sent():
            @pl.loop(0, 4)
            def _(i):
                relay_copy(s, i).wait_send()

        leaving["relay", s] = sent

    def near_stage(s, j):
        for way in (1, 0):
            if j == 0:
                core_copy(s, 1 + 2 * way).wait_recv()
            i = j + 2 - 2 * way
            encode(pair_sum(s, 1 + 2 * way, (zl + 1 + i) % 4), xs.at[s, way, i])
            x_copy(s, way, i).start()
        leaving["near", s, j] = lambda: wait_sent([x_copy(s, 1, j), x_copy(s, 0, j + 2)])

    def relayed_stage(s, j):
        for way in (0, 1):
            i = j + 2 * way
            own = pair_sum(s, 1 + 2 * way, (zl + 1 + i) % 4)
            relay_copy(s, i).wait_recv()
            encode(own + decode(xqr.at[s, i]), xs.at[s, way, i])
            x_copy(s, way, i).start()
        leaving["relayed", s, j] = lambda: wait_sent([x_copy(s, 0, j), x_copy(s, 1, j + 2)])

    def x_sum(s, i):
        total = pair_sum(s, 0, (zl + 1 + i) % 4)
        for way in range(2):
            x_copy(s, way, i).wait_recv()
            total += decode(xr.at[s, way, i])
        return total

    def z_send(s, dz):
        if dz == 1:
            core_copy(s, 0).wait_recv()
        encode(x_sum(s, dz - 1), zs.at[s, dz - 1])
        z_copy(s, dz).start()
        leaving["z", s, dz] = lambda: z_copy(s, dz).wait_send()

    def z_keep(s):
        za[s] = x_sum(s, 3)

    def g_stage(s):
        total = za[s]
        for dz in range(1, 4):
            z_copy(s, dz).wait_recv()
            total += decode(zr.at[s, dz - 1])
        turned = total.T
        a, b = turned[0:64], turned[64:128]
        gslab[s, :, 0:256] = a
        gslab[s, :, 256:512] = b
        encode(jnp.concatenate([a[:, :128], a[:, 128:], b[:, :128], b[:, 128:]], axis=0), ag.at[s, t])
        start(g_copies[s][0])
        leaving["g", s] = lambda: wait_sent(g_copies[s][0])

    def forward(name, s, copies):
        copies[0][0].wait_recv()
        start(copies[1])
        leaving["forward", name, s] = lambda: wait_sent(copies[1])

    def unpack(message, s, store, half):
        @pl.loop(0, 4)
        def _(j):
            k = half * 4 + j
            v = decode(message(k))
            rows = pl.ds(pl.multiple_of(k * 64, 64), 64)
            for q in range(4):
                high, low = split(v[q * 64 : q * 64 + 64])
                store[s, 0, rows, q * 128 : q * 128 + 128] = high
                store[s, 1, rows, q * 128 : q * 128 + 128] = low

    def half_product(a, store, s, half):
        k = pl.ds(pl.multiple_of(half * 256, 256), 256)
        return dot3(a[:, k], store[s, 0, k, :], store[s, 1, k, :], PLAIN)

    def near_half(copies, messages, s, store, a):
        for cp in copies[0][1:]:
            cp.wait_recv()
        unpack(lambda k: messages.at[s, k], s, store, zh)
        part[s] = half_product(a, store, s, zh)

    def far_half(copies, messages, s, store, a):
        for cp in copies[1]:
            cp.wait_recv()
        unpack(lambda k: messages.at[s, k], s, store, 1 - zh)
        return part[s] + half_product(a, store, s, 1 - zh)

    def put(ref, dst, i, s):
        return pltpu.make_async_copy(ref.at[s], dst.at[s], out_sem.at[i, s])

    def rotate_near(s):
        near_half(g_copies[s], ag, s, gt, br.at[s])

    def rotate(s):
        partial = far_half(g_copies[s], ag, s, gt, br.at[s])
        rotated = dot3(partial, left[s, 0], left[s, 1], MINOR)
        new_moment = first_decay * mo[s] + (1.0 - first_decay) * rotated
        new_second = second_decay * se[s] + (1.0 - second_decay) * rotated * rotated
        mo[s] = new_moment
        se[s] = new_second
        direction = new_moment / (jnp.sqrt(new_second) + epsilon)
        half = dot3(direction, left[s, 0], left[s, 1], PLAIN)
        encode(stacked(half), ah.at[s, t])
        start(h_copies[s][0])
        leaving["h", s] = lambda: wait_sent(h_copies[s][0])
        put(mo, nm, 0, s).start()
        put(se, ns, 1, s).start()

    def statistics(s):
        right = dot3(gslab[s], gt[s, 0], gt[s, 1], MINOR)
        sr[s] = second_decay * sr[s] + (1.0 - second_decay) * right
        put(sr, nr, 2, s).start()
        cols = pl.ds(pl.multiple_of((t // 2) * 128, 128), 128)
        rows = gt[s, 0, :, cols].astype(f32) + gt[s, 1, :, cols].astype(f32)
        tmp[...] = rows.T
        mine = tmp[pl.ds(pl.multiple_of((t % 2) * 64, 64), 64), :]
        out = dot3(mine, gt[s, 0], gt[s, 1], PLAIN)
        sl[s] = second_decay * sl[s] + (1.0 - second_decay) * out
        put(sl, nl, 3, s).start()

    def back_near(s):
        near_half(h_copies[s], ah, s, hb, rct.at[pl.ds(s * 64, 64)])

    def back(s):
        bk[pl.ds(s * 64, 64), :] = far_half(h_copies[s], ah, s, hb, rct.at[pl.ds(s * 64, 64)])

    def grad_ready():
        @pl.loop(0, 8)
        def _(i):
            grad_load(i).wait()

    def right_ready():
        @pl.loop(1, 8)
        def _(d):
            right_copy(d).wait_recv()

        rct[...] = jnp.concatenate([rc[k, 0].astype(f32) + rc[k, 1].astype(f32) for k in range(8)], axis=0).T

    def left_ready():
        for cp in loads[1:]:
            cp.wait()
        for cp in left_first[1:] + left_second:
            cp.wait_recv()
        for s in range(2):
            unpack(lambda k: lm.at[k, s], s, left, 0)
            unpack(lambda k: lm.at[k, s], s, left, 1)

    def send_back():
        rows = bk[...].T.astype(bf16)
        for k in range(32):
            a2s[k] = rows[k * 16 : k * 16 + 16]

        @pl.loop(0, 31)
        def _(d):
            a2a_copy((d + 15) % 31 + 1).start()

        a2r[f] = a2s[f]

    steps = [
        lambda: grad_ready(),
        lambda: core_part(0, 2),
        lambda: core_part(0, 3),
        lambda: core_part(0, 1),
        lambda: send_left(),
        lambda: relay_stage(0),
        lambda: core_part(0, 0),
        lambda: core_part(1, 2),
        lambda: near_stage(0, 0),
        lambda: near_stage(0, 1),
        lambda: core_part(1, 3),
        lambda: relayed_stage(0, 0),
        lambda: relayed_stage(0, 1),
        lambda: core_part(1, 1),
        lambda: left_device("near", 0, 0),
        lambda: left_device("near", 0, 1),
        lambda: relay_stage(1),
        lambda: core_part(1, 0),
        lambda: z_send(0, 1),
        lambda: z_send(0, 3),
        lambda: z_send(0, 2),
        lambda: z_keep(0),
        lambda: near_stage(1, 0),
        lambda: near_stage(1, 1),
        lambda: relayed_stage(1, 0),
        lambda: relayed_stage(1, 1),
        lambda: forward("left", 0, (left_first, left_second)),
        lambda: g_stage(0),
        lambda: z_send(1, 1),
        lambda: z_send(1, 3),
        lambda: z_send(1, 2),
        lambda: z_keep(1),
        lambda: left_ready(),
        lambda: forward("g", 0, g_copies[0]),
        lambda: rotate_near(0),
        lambda: g_stage(1),
        lambda: rotate(0),
        lambda: forward("g", 1, g_copies[1]),
        lambda: send_right(),
        lambda: rotate_near(1),
        lambda: rotate(1),
        lambda: forward("h", 0, h_copies[0]),
        lambda: statistics(0),
        lambda: right_ready(),
        lambda: forward("h", 1, h_copies[1]),
        lambda: back_near(0),
        lambda: back(0),
        lambda: statistics(1),
        lambda: back_near(1),
        lambda: back(1),
        lambda: send_back(),
    ]
    for step in steps:
        step()

    for sent in list(leaving.values()):
        sent()
    for s in range(2):
        for i, (ref, dst) in enumerate(((mo, nm), (se, ns), (sr, nr), (sl, nl))):
            put(ref, dst, i, s).wait()

    @pl.loop(1, 32)
    def _(d):
        a2a_copy(d).wait()


def finish(bos, rows, nl, nr, nm, ns, upd_out, nl_out, nr_out, nm_out, ns_out, upd, sem):
    outs = [
        pltpu.make_async_copy(src, dst, sem.at[i])
        for i, (src, dst) in enumerate(((nl, nl_out), (nr, nr_out), (nm, nm_out), (ns, ns_out), (upd, upd_out)))
    ]
    for out in outs[:4]:
        out.start()

    upper = lane_iota(16) >= 64

    @pl.loop(0, 16)
    def _(k):
        for u in range(2):
            both = rows[2 * k + u].astype(f32)
            turned = roll_half(both)
            for j in range(2):
                b = bos[4 * k + 2 * u + j]
                half = b % 2
                cols = pl.ds(pl.multiple_of(b % 16 // 2 * 128, 128), 128)
                old = upd[b // 16, :, cols]
                new = jnp.where((lane_iota(16) * 0 + half) == j, both, turned).astype(bf16)
                upd[b // 16, :, cols] = jnp.where(upper == ((lane_iota(16) * 0 + half) == 1), new, old)

    outs[4].start()
    for out in outs:
        out.wait()


def local(grad_part, block_of_slot, stat_left, stat_right, basis_left, basis_right, moment, second):
    smem = pl.BlockSpec(memory_space=pltpu.SMEM)
    hbm = pl.BlockSpec(memory_space=pl.ANY)
    state = jax.ShapeDtypeStruct((2, 64, 512), f32)
    vmem = pl.BlockSpec(memory_space=pltpu.VMEM)
    v = pltpu.VMEM
    dma = pltpu.SemaphoreType.DMA
    outs = pl.pallas_call(
        kernel,
        name="step",
        out_shape=(jax.ShapeDtypeStruct((32, 16, 128), bf16), state, state, state, state),
        in_specs=[smem] + [hbm] * 7,
        out_specs=(vmem, hbm, hbm, hbm, hbm),
        scratch_shapes=[
            v((64, 256, 128), f32),
            *[v((2, 64, 512), f32)] * 6,
            v((2, 4, 4, 256, 128), f32),
            v((2, 4, 4, 256, 128), f32),
            v((2, 4, 272, 128), i16),
            v((2, 4, 272, 128), i16),
            v((2, 2, 4, 272, 128), i16),
            v((2, 2, 4, 272, 128), i16),
            v((2, 3, 272, 128), i16),
            v((2, 3, 272, 128), i16),
            v((2, 256, 128), f32),
            v((2, 64, 512), f32),
            v((2, 8, 272, 128), i16),
            v((2, 8, 272, 128), i16),
            v((8, 2, 272, 128), i16),
            v((2, 2, 512, 512), bf16),
            v((8, 2, 64, 128), bf16),
            v((8, 2, 64, 128), bf16),
            v((128, 512), f32),
            v((2, 2, 512, 512), bf16),
            v((2, 2, 512, 512), bf16),
            v((128, 512), f32),
            v((128, 512), f32),
            v((2, 64, 512), f32),
            v((32, 16, 128), bf16),
            dma((6,)),
            dma((8,)),
            dma((4, 2)),
            *[dma((2, 4))] * 4,
            *[dma((2, 2, 4))] * 2,
            *[dma((2, 3))] * 2,
            *[dma((7,))] * 2,
            *[dma((8,))] * 2,
            *[dma((2, 7))] * 4,
            *[dma((32,))] * 2,
        ],
        compiler_params=pltpu.CompilerParams(
            collective_id=0, has_side_effects=True, vmem_limit_bytes=vmem_bytes
        ),
    )(block_of_slot, grad_part.reshape(8, 256, 1024), stat_left, stat_right, basis_left, basis_right, moment, second)
    return pl.pallas_call(
        finish,
        name="finish",
        out_shape=(jax.ShapeDtypeStruct((4, 16, 1024), bf16), state, state, state, state),
        in_specs=[smem] + [vmem] * 5,
        out_specs=(hbm,) * 5,
        scratch_shapes=[v((4, 16, 1024), bf16), dma((5,))],
        compiler_params=pltpu.CompilerParams(vmem_limit_bytes=vmem_bytes),
    )(block_of_slot, *outs)


def solution(mesh):
    return jax.shard_map(
        local,
        mesh=mesh,
        in_specs=(
            P("fsdp", None, None, "tp"),
            P(),
            P("fsdp", "tp", None),
            P("fsdp", "tp", None),
            P("fsdp", "tp", None),
            P("fsdp", "tp", None),
            P("fsdp", "tp", None),
            P("fsdp", "tp", None),
        ),
        out_specs=(
            P(None, "fsdp", "tp"),
            P("fsdp", "tp", None),
            P("fsdp", "tp", None),
            P("fsdp", "tp", None),
            P("fsdp", "tp", None),
        ),
        check_vma=False,
    )
```

```python
import jax
import jax.numpy as jnp
from jax import lax
from jax.experimental import pallas as pl
from jax.experimental.pallas import tpu as pltpu
from jax.sharding import PartitionSpec as P

first_decay = 0.9
second_decay = 0.95
epsilon = 1e-08
MESH = pl.DeviceIdType.MESH
f32, bf16, i16, i32 = jnp.float32, jnp.bfloat16, jnp.int16, jnp.int32
FAR = (2, 1, 3)
vmem_bytes = 64 * 2**20 - 19 * 2**16


def roll_half(v):
    return pltpu.roll(v, 64, 1)


def lane_iota(rows):
    return lax.broadcasted_iota(i32, (rows, 128), 1)


def split(v):
    high = v.astype(bf16)
    return high, (v - high.astype(f32)).astype(bf16)


def dot(a, b, dims):
    return lax.dot_general(a, b, (dims, ((), ())), preferred_element_type=f32)


PLAIN = ((1,), (0,))
MINOR = ((1,), (1,))


def dot3(a, bh, bl, dims):
    ah, al = split(a)
    return dot(ah, bh, dims) + (dot(ah, bl, dims) + dot(al, bh, dims))


def encode(v, ref):
    top = jnp.max(jnp.abs(v), axis=0, keepdims=True)
    power = jnp.ceil(jnp.log2(jnp.maximum(top, 1e-30) * (1.0 / 32500.0)))
    ref[pl.ds(0, 256), :] = jnp.round(v * jnp.exp2(-power)).astype(i32).astype(i16)
    ref[pl.ds(256, 16), :] = jnp.broadcast_to(power, (16, 128)).astype(i32).astype(i16)


def scale_of(ref):
    return jnp.exp2(ref[pl.ds(256, 16), :].astype(i32).astype(f32))[0:1]


def decode(ref):
    return ref[pl.ds(0, 256), :].astype(i32).astype(f32) * scale_of(ref)


def kernel(
    bos, grad_h, sl_h, sr_h, bl_h, br_h, mo_h, se_h,
    a2r, nl, nr, nm, ns,
    g, sl, sr, bl, br, mo, se,
    cs, cr, xq, xqr, xs, xr, zs, zr, za, gslab, ag, ah, lm, left, rmsg, rc, rct, gt, hb, tmp, bk, part, pb, pbr, a2s,
    loc, g_sem, out_sem, c_s, c_r, q_s, q_r, x_s, x_r, z_s, z_r, l_s, l_r, r_s, r_r, g_s, g_r, h_s, h_r, p_s, p_r, a_s, a_r,
):
    f = lax.axis_index("fsdp")
    t = lax.axis_index("tp")
    x, zl, c = f // 8, (f // 2) % 4, f % 2
    zh, y = t // 4, t % 4

    def fdev(x_, z_, c_):
        return ((x_ * 4 + z_) * 2 + c_, t)

    def tdev(zh_, y_):
        return (f, zh_ * 4 + y_)

    def remote(src, dst, ss, rs, dev):
        return pltpu.make_async_remote_copy(
            src_ref=src, dst_ref=dst, send_sem=ss, recv_sem=rs, device_id=dev, device_id_type=MESH
        )

    loads = [
        pltpu.make_async_copy(src, dst, loc.at[i])
        for i, (src, dst) in enumerate(((bl_h, bl), (br_h, br), (sl_h, sl), (sr_h, sr), (mo_h, mo), (se_h, se)))
    ]

    def grad_load(i):
        return pltpu.make_async_copy(
            grad_h.at[:, :, pl.ds(pl.multiple_of(i * 128, 128), 128)], g.at[pl.ds(8 * i, 8)], g_sem.at[i]
        )

    @pl.loop(0, 8)
    def _(i):
        grad_load(i).start()

    for cp in loads:
        cp.start()

    barrier = pltpu.get_barrier_semaphore()

    @pl.loop(1, 32)
    def _(d):
        pl.semaphore_signal(barrier, inc=1, device_id=((f + d) % 32, t), device_id_type=MESH)

    for peer in [tdev(1 - zh, y)] + [tdev(zh, (y + d) % 4) for d in FAR]:
        pl.semaphore_signal(barrier, inc=1, device_id=peer, device_id_type=MESH)

    def core_copy(s, dx):
        return remote(cs.at[s, dx], cr.at[s, dx], c_s.at[s, dx], c_r.at[s, dx], fdev(x, zl, 1 - c))

    def relay_copy(s, i):
        return remote(
            xq.at[s, i], xqr.at[s, i], q_s.at[s, i], q_r.at[s, i], fdev((x + 1 + i // 2 * 2) % 4, zl, c)
        )

    def x_copy(s, way, i):
        return remote(
            xs.at[s, way, i], xr.at[s, way, i], x_s.at[s, way, i], x_r.at[s, way, i],
            fdev((x + 1 + 2 * way) % 4, zl, c),
        )

    def z_copy(s, dz):
        return remote(
            zs.at[s, dz - 1], zr.at[s, dz - 1], z_s.at[s, dz - 1], z_r.at[s, dz - 1],
            fdev(x, (zl + dz) % 4, c),
        )

    def tp_copies(view, ss, rs):
        own = view(t)
        other = view((1 - zh) * 4 + y)
        first = [remote(own, own, ss(0), rs(0), tdev(1 - zh, y))]
        first += [remote(own, own, ss(d), rs(d), tdev(zh, (y + d) % 4)) for d in FAR]
        second = [remote(other, other, ss(3 + d), rs(3 + d), tdev(zh, (y + d) % 4)) for d in FAR]
        return first, second

    left_first, left_second = tp_copies(lambda k: lm.at[k], lambda i: l_s.at[i], lambda i: l_r.at[i])
    g_copies = [
        tp_copies(lambda k, s=s: ag.at[s, k], lambda i, s=s: g_s.at[s, i], lambda i, s=s: g_r.at[s, i])
        for s in range(2)
    ]
    h_copies = [
        [
            remote(ah.at[s, t], ah.at[s, t], h_s.at[s, d - 1], h_r.at[s, d - 1], tdev(zh, (y + d) % 4))
            for d in FAR
        ]
        for s in range(2)
    ]
    p_copies = [remote(pb.at[s], pbr.at[s], p_s.at[s], p_r.at[s], tdev(1 - zh, y)) for s in range(2)]
    right_copies = [
        remote(rmsg.at[(y + d) % 4], rc.at[y], r_s.at[d - 1], r_r.at[d - 1], tdev(zh, (y + d) % 4)) for d in FAR
    ]

    def a2a_copy(d):
        k = (f + d) % 32
        return remote(a2s.at[k], a2r.at[f], a_s.at[d], a_r.at[d], (k, t))

    def start(copies):
        for cp in copies:
            cp.start()

    leaving = {}

    def left_device(*name):
        leaving.pop(name)()

    def wait_sent(copies):
        for cp in copies:
            cp.wait_send()

    pl.semaphore_wait(barrier, 35)

    def stacked(v):
        return jnp.concatenate([v[:, q * 128 : q * 128 + 128] for q in range(4)], axis=0)

    def send_left():
        loads[0].wait()
        for s in range(2):
            encode(stacked(bl[s]), lm.at[t, s])
        start(left_first)
        leaving["left", 0] = lambda: wait_sent(left_first)

    def send_right():
        loads[1].wait()
        lanes = lane_iota(64)
        for u in range(4):
            a = br[0, :, u * 128 : u * 128 + 128]
            b = br[1, :, u * 128 : u * 128 + 128]
            even, odd = jnp.where(lanes < 64, a, roll_half(b)), jnp.where(lanes < 64, roll_half(a), b)
            for k, v in ((2 * u, even), (2 * u + 1, odd)):
                high, low = split(v)
                rmsg[k % 4, k // 4, 0] = high
                rmsg[k % 4, k // 4, 1] = low
        rc[y] = rmsg[y]
        start(right_copies)
        leaving["right", 0] = lambda: wait_sent(right_copies)

    def extract(slot):
        b = bos[slot]
        half = b % 2
        first = ((b % 16) // 2 * 4 + b // 16) * 2
        near = g[first + half]
        away = g[first + 1 - half]
        upper = (lane_iota(256) >= 64).astype(i32)
        return jnp.where(upper == half, near, roll_half(away))

    def slot_of(s, dx, z, core):
        return ((((x + dx) % 4) * 4 + z) * 2 + core) * 2 + s

    def core_part(s, dx):
        @pl.loop(0, 4)
        def _(z):
            cs[s, dx, z] = extract(slot_of(s, dx, z, 1 - c))

        core_copy(s, dx).start()
        leaving["core", s, dx] = lambda: core_copy(s, dx).wait_send()

    def pair_sum(s, dx, z):
        return extract(slot_of(s, dx, z, c)) + cr[s, dx, z]

    def relay_stage(s):
        core_copy(s, 2).wait_recv()

        @pl.loop(0, 4)
        def _(j):
            i = j // 2 + 2 * (j % 2)
            encode(pair_sum(s, 2, (zl + 1 + i) % 4), xq.at[s, i])
            relay_copy(s, i).start()

        def sent():
            @pl.loop(0, 4)
            def _(i):
                relay_copy(s, i).wait_send()

        leaving["relay", s] = sent

    def near_stage(s, j):
        for way in (1, 0):
            if j == 0:
                core_copy(s, 1 + 2 * way).wait_recv()
            i = j + 2 - 2 * way
            encode(pair_sum(s, 1 + 2 * way, (zl + 1 + i) % 4), xs.at[s, way, i])
            x_copy(s, way, i).start()
        leaving["near", s, j] = lambda: wait_sent([x_copy(s, 1, j), x_copy(s, 0, j + 2)])

    def relayed_stage(s, j):
        for way in (0, 1):
            i = j + 2 * way
            own = pair_sum(s, 1 + 2 * way, (zl + 1 + i) % 4)
            relay_copy(s, i).wait_recv()
            encode(own + decode(xqr.at[s, i]), xs.at[s, way, i])
            x_copy(s, way, i).start()
        leaving["relayed", s, j] = lambda: wait_sent([x_copy(s, 0, j), x_copy(s, 1, j + 2)])

    def x_sum(s, i):
        total = pair_sum(s, 0, (zl + 1 + i) % 4)
        for way in range(2):
            x_copy(s, way, i).wait_recv()
            total += decode(xr.at[s, way, i])
        return total

    def z_send(s, dz):
        if dz == 1:
            core_copy(s, 0).wait_recv()
        encode(x_sum(s, dz - 1), zs.at[s, dz - 1])
        z_copy(s, dz).start()
        leaving["z", s, dz] = lambda: z_copy(s, dz).wait_send()

    def z_keep(s):
        za[s] = x_sum(s, 3)

    def g_stage(s):
        total = za[s]
        for dz in range(1, 4):
            z_copy(s, dz).wait_recv()
            total += decode(zr.at[s, dz - 1])
        turned = total.T
        a, b = turned[0:64], turned[64:128]
        gslab[s, :, 0:256] = a
        gslab[s, :, 256:512] = b
        encode(jnp.concatenate([a[:, :128], a[:, 128:], b[:, :128], b[:, 128:]], axis=0), ag.at[s, t])
        start(g_copies[s][0])
        leaving["g", s] = lambda: wait_sent(g_copies[s][0])

    def forward(name, s, copies):
        copies[0][0].wait_recv()
        start(copies[1])
        leaving["forward", name, s] = lambda: wait_sent(copies[1])

    def unpack(message, s, store, half):
        @pl.loop(0, 4)
        def _(j):
            k = half * 4 + j
            v = decode(message(k))
            rows = pl.ds(pl.multiple_of(k * 64, 64), 64)
            for q in range(4):
                high, low = split(v[q * 64 : q * 64 + 64])
                store[s, 0, rows, q * 128 : q * 128 + 128] = high
                store[s, 1, rows, q * 128 : q * 128 + 128] = low

    def half_product(a, store, s, half):
        k = pl.ds(pl.multiple_of(half * 256, 256), 256)
        return dot3(a(k), store[s, 0, k, :], store[s, 1, k, :], PLAIN)

    def near_half(copies, messages, s, store, a):
        for cp in copies:
            cp.wait_recv()
        unpack(lambda k: messages.at[s, k], s, store, zh)
        return half_product(a, store, s, zh)

    def far_half(copies, messages, s, store, a):
        for cp in copies:
            cp.wait_recv()
        unpack(lambda k: messages.at[s, k], s, store, 1 - zh)
        return half_product(a, store, s, 1 - zh)

    def put(ref, dst, i, s):
        return pltpu.make_async_copy(ref.at[s], dst.at[s], out_sem.at[i, s])

    def rotate_near(s):
        part[s] = near_half(g_copies[s][0][1:], ag, s, gt, lambda k: br[s, :, k])

    def rotate(s):
        partial = part[s] + far_half(g_copies[s][1], ag, s, gt, lambda k: br[s, :, k])
        rotated = dot3(partial, left[s, 0], left[s, 1], MINOR)
        new_moment = first_decay * mo[s] + (1.0 - first_decay) * rotated
        new_second = second_decay * se[s] + (1.0 - second_decay) * rotated * rotated
        mo[s] = new_moment
        se[s] = new_second
        direction = new_moment / (jnp.sqrt(new_second) + epsilon)
        half = dot3(direction, left[s, 0], left[s, 1], PLAIN)
        encode(stacked(half), ah.at[s, t])
        start(h_copies[s])
        leaving["h", s] = lambda: wait_sent(h_copies[s])
        put(mo, nm, 0, s).start()
        put(se, ns, 1, s).start()

    def statistics(s):
        right = dot3(gslab[s], gt[s, 0], gt[s, 1], MINOR)
        sr[s] = second_decay * sr[s] + (1.0 - second_decay) * right
        put(sr, nr, 2, s).start()
        cols = pl.ds(pl.multiple_of((t // 2) * 128, 128), 128)
        rows = gt[s, 0, :, cols].astype(f32) + gt[s, 1, :, cols].astype(f32)
        tmp[...] = rows.T
        mine = tmp[pl.ds(pl.multiple_of((t % 2) * 64, 64), 64), :]
        out = dot3(mine, gt[s, 0], gt[s, 1], PLAIN)
        sl[s] = second_decay * sl[s] + (1.0 - second_decay) * out
        put(sl, nl, 3, s).start()

    def back_near(s):
        rows = pl.ds(s * 64, 64)
        both = near_half(
            h_copies[s], ah, s, hb, lambda k: jnp.concatenate([rct[1 - zh, rows, :], rct[zh, rows, :]], axis=0)
        )
        encode(stacked(both[0:64]), pb.at[s])
        p_copies[s].start()
        leaving["p", s] = lambda: p_copies[s].wait_send()
        bk[rows, :] = both[64:128]

    def back(s):
        p_copies[s].wait_recv()
        other = decode(pbr.at[s])
        for q in range(4):
            bk[s * 64 : s * 64 + 64, q * 128 : q * 128 + 128] += other[q * 64 : q * 64 + 64]

    def grad_ready():
        @pl.loop(0, 8)
        def _(i):
            grad_load(i).wait()

    def right_ready():
        for cp in right_copies:
            cp.wait_recv()
        for h in range(2):
            rct[h] = jnp.concatenate([rc[k, h, 0].astype(f32) + rc[k, h, 1].astype(f32) for k in range(4)], axis=0).T

    def left_ready():
        for cp in loads[2:]:
            cp.wait()
        for cp in left_first[1:] + left_second:
            cp.wait_recv()
        for s in range(2):
            unpack(lambda k: lm.at[k, s], s, left, 0)
            unpack(lambda k: lm.at[k, s], s, left, 1)

    def send_back():
        rows = bk[...].T.astype(bf16)
        for k in range(32):
            a2s[k] = rows[k * 16 : k * 16 + 16]

        @pl.loop(0, 31)
        def _(d):
            a2a_copy((d + 15) % 31 + 1).start()

        a2r[f] = a2s[f]

    steps = [
        lambda: grad_ready(),
        lambda: core_part(0, 2),
        lambda: core_part(0, 3),
        lambda: core_part(0, 1),
        lambda: send_left(),
        lambda: relay_stage(0),
        lambda: send_right(),
        lambda: core_part(0, 0),
        lambda: core_part(1, 2),
        lambda: near_stage(0, 0),
        lambda: near_stage(0, 1),
        lambda: core_part(1, 3),
        lambda: relayed_stage(0, 0),
        lambda: relayed_stage(0, 1),
        lambda: core_part(1, 1),
        lambda: left_device("near", 0, 0),
        lambda: left_device("near", 0, 1),
        lambda: relay_stage(1),
        lambda: core_part(1, 0),
        lambda: z_send(0, 1),
        lambda: z_send(0, 3),
        lambda: z_send(0, 2),
        lambda: z_keep(0),
        lambda: near_stage(1, 0),
        lambda: near_stage(1, 1),
        lambda: relayed_stage(1, 0),
        lambda: relayed_stage(1, 1),
        lambda: forward("left", 0, (left_first, left_second)),
        lambda: g_stage(0),
        lambda: z_send(1, 1),
        lambda: z_send(1, 3),
        lambda: z_send(1, 2),
        lambda: z_keep(1),
        lambda: left_ready(),
        lambda: forward("g", 0, g_copies[0]),
        lambda: rotate_near(0),
        lambda: g_stage(1),
        lambda: rotate(0),
        lambda: forward("g", 1, g_copies[1]),
        lambda: rotate_near(1),
        lambda: right_ready(),
        lambda: back_near(0),
        lambda: rotate(1),
        lambda: statistics(0),
        lambda: back_near(1),
        lambda: back(0),
        lambda: statistics(1),
        lambda: back(1),
        lambda: send_back(),
    ]
    for step in steps:
        step()

    for sent in list(leaving.values()):
        sent()
    for s in range(2):
        for i, (ref, dst) in enumerate(((mo, nm), (se, ns), (sr, nr), (sl, nl))):
            put(ref, dst, i, s).wait()

    @pl.loop(1, 32)
    def _(d):
        a2a_copy(d).wait()


def finish(bos, rows, nl, nr, nm, ns, upd_out, nl_out, nr_out, nm_out, ns_out, upd, sem):
    outs = [
        pltpu.make_async_copy(src, dst, sem.at[i])
        for i, (src, dst) in enumerate(((nl, nl_out), (nr, nr_out), (nm, nm_out), (ns, ns_out), (upd, upd_out)))
    ]
    for out in outs[:4]:
        out.start()

    upper = lane_iota(16) >= 64

    for k in range(32):
        both = rows[k].astype(f32)
        turned = roll_half(both)
        for j in range(2):
            b = bos[2 * k + j]
            half = b & 1
            cols = pl.ds(pl.multiple_of(((b & 15) >> 1) * 128, 128), 128)
            old = upd[b >> 4, :, cols]
            new = jnp.where((lane_iota(16) * 0 + half) == j, both, turned).astype(bf16)
            upd[b >> 4, :, cols] = jnp.where(upper == ((lane_iota(16) * 0 + half) == 1), new, old)

    outs[4].start()
    for out in outs:
        out.wait()


def local(grad_part, block_of_slot, stat_left, stat_right, basis_left, basis_right, moment, second):
    smem = pl.BlockSpec(memory_space=pltpu.SMEM)
    hbm = pl.BlockSpec(memory_space=pl.ANY)
    state = jax.ShapeDtypeStruct((2, 64, 512), f32)
    vmem = pl.BlockSpec(memory_space=pltpu.VMEM)
    v = pltpu.VMEM
    dma = pltpu.SemaphoreType.DMA
    outs = pl.pallas_call(
        kernel,
        name="step",
        out_shape=(jax.ShapeDtypeStruct((32, 16, 128), bf16), state, state, state, state),
        in_specs=[smem] + [hbm] * 7,
        out_specs=(vmem, hbm, hbm, hbm, hbm),
        scratch_shapes=[
            v((64, 256, 128), f32),
            *[v((2, 64, 512), f32)] * 6,
            v((2, 4, 4, 256, 128), f32),
            v((2, 4, 4, 256, 128), f32),
            v((2, 4, 272, 128), i16),
            v((2, 4, 272, 128), i16),
            v((2, 2, 4, 272, 128), i16),
            v((2, 2, 4, 272, 128), i16),
            v((2, 3, 272, 128), i16),
            v((2, 3, 272, 128), i16),
            v((2, 256, 128), f32),
            v((2, 64, 512), f32),
            v((2, 8, 272, 128), i16),
            v((2, 8, 272, 128), i16),
            v((8, 2, 272, 128), i16),
            v((2, 2, 512, 512), bf16),
            v((4, 2, 2, 64, 128), bf16),
            v((4, 2, 2, 64, 128), bf16),
            v((2, 128, 256), f32),
            v((2, 2, 512, 512), bf16),
            v((2, 2, 512, 512), bf16),
            v((128, 512), f32),
            v((128, 512), f32),
            v((2, 64, 512), f32),
            v((2, 272, 128), i16),
            v((2, 272, 128), i16),
            v((32, 16, 128), bf16),
            dma((6,)),
            dma((8,)),
            dma((4, 2)),
            *[dma((2, 4))] * 4,
            *[dma((2, 2, 4))] * 2,
            *[dma((2, 3))] * 2,
            *[dma((7,))] * 2,
            *[dma((3,))] * 2,
            *[dma((2, 7))] * 2,
            *[dma((2, 3))] * 2,
            *[dma((2,))] * 2,
            *[dma((32,))] * 2,
        ],
        compiler_params=pltpu.CompilerParams(
            collective_id=0, has_side_effects=True, vmem_limit_bytes=vmem_bytes
        ),
    )(block_of_slot, grad_part.reshape(8, 256, 1024), stat_left, stat_right, basis_left, basis_right, moment, second)
    return pl.pallas_call(
        finish,
        name="finish",
        out_shape=(jax.ShapeDtypeStruct((4, 16, 1024), bf16), state, state, state, state),
        in_specs=[smem] + [vmem] * 5,
        out_specs=(hbm,) * 5,
        scratch_shapes=[v((4, 16, 1024), bf16), dma((5,))],
        compiler_params=pltpu.CompilerParams(vmem_limit_bytes=vmem_bytes),
    )(block_of_slot, *outs)


def solution(mesh):
    return jax.shard_map(
        local,
        mesh=mesh,
        in_specs=(
            P("fsdp", None, None, "tp"),
            P(),
            P("fsdp", "tp", None),
            P("fsdp", "tp", None),
            P("fsdp", "tp", None),
            P("fsdp", "tp", None),
            P("fsdp", "tp", None),
            P("fsdp", "tp", None),
        ),
        out_specs=(
            P(None, "fsdp", "tp"),
            P("fsdp", "tp", None),
            P("fsdp", "tp", None),
            P("fsdp", "tp", None),
            P("fsdp", "tp", None),
        ),
        check_vma=False,
    )
```

```python
import jax
import jax.numpy as jnp
from jax import lax
from jax.experimental import pallas as pl
from jax.experimental.pallas import tpu as pltpu
from jax.sharding import PartitionSpec as P

first_decay = 0.9
second_decay = 0.95
epsilon = 1e-08
MESH = pl.DeviceIdType.MESH
f32, bf16, i16, i32 = jnp.float32, jnp.bfloat16, jnp.int16, jnp.int32
FAR = (2, 1, 3)
vmem_bytes = 64 * 2**20 - 19 * 2**16


def roll_half(v):
    return pltpu.roll(v, 64, 1)


def lane_iota(rows):
    return lax.broadcasted_iota(i32, (rows, 128), 1)


def split(v):
    high = v.astype(bf16)
    return high, (v - high.astype(f32)).astype(bf16)


def dot(a, b, dims):
    return lax.dot_general(a, b, (dims, ((), ())), preferred_element_type=f32)


PLAIN = ((1,), (0,))
MINOR = ((1,), (1,))


def dot3(a, bh, bl, dims):
    ah, al = split(a)
    return dot(ah, bh, dims) + (dot(ah, bl, dims) + dot(al, bh, dims))


def encode(v, ref):
    top = jnp.max(jnp.abs(v), axis=0, keepdims=True)
    power = jnp.ceil(jnp.log2(jnp.maximum(top, 1e-30) * (1.0 / 32500.0)))
    ref[pl.ds(0, 256), :] = jnp.round(v * jnp.exp2(-power)).astype(i32).astype(i16)
    ref[pl.ds(256, 16), :] = jnp.broadcast_to(power, (16, 128)).astype(i32).astype(i16)


def scale_of(ref):
    return jnp.exp2(ref[pl.ds(256, 16), :].astype(i32).astype(f32))[0:1]


def decode(ref):
    return ref[pl.ds(0, 256), :].astype(i32).astype(f32) * scale_of(ref)


def kernel(
    bos, grad_h, sl_h, sr_h, bl_h, br_h, mo_h, se_h,
    a2r, nl, nr, nm, ns,
    g, sl, sr, bl, br, mo, se,
    cs, cr, xq, xqr, xs, xr, zs, zr, za, gslab, ag, ah, lm, left, rmsg, rc, rct, gt, hb, tmp, bk, part, pb, pbr, a2s,
    loc, g_sem, out_sem, c_s, c_r, q_s, q_r, x_s, x_r, z_s, z_r, l_s, l_r, r_s, r_r, g_s, g_r, h_s, h_r, p_s, p_r, a_s, a_r,
):
    f = lax.axis_index("fsdp")
    t = lax.axis_index("tp")
    x, zl, c = f // 8, (f // 2) % 4, f % 2
    zh, y = t // 4, t % 4

    def fdev(x_, z_, c_):
        return ((x_ * 4 + z_) * 2 + c_, t)

    def tdev(zh_, y_):
        return (f, zh_ * 4 + y_)

    def remote(src, dst, ss, rs, dev):
        return pltpu.make_async_remote_copy(
            src_ref=src, dst_ref=dst, send_sem=ss, recv_sem=rs, device_id=dev, device_id_type=MESH
        )

    loads = [
        pltpu.make_async_copy(src, dst, loc.at[i])
        for i, (src, dst) in enumerate(((bl_h, bl), (br_h, br), (sl_h, sl), (sr_h, sr), (mo_h, mo), (se_h, se)))
    ]

    def grad_load(i):
        return pltpu.make_async_copy(
            grad_h.at[:, :, pl.ds(pl.multiple_of(i * 128, 128), 128)], g.at[pl.ds(8 * i, 8)], g_sem.at[i]
        )

    @pl.loop(0, 8)
    def _(i):
        grad_load(i).start()

    for cp in loads:
        cp.start()

    barrier = pltpu.get_barrier_semaphore()

    @pl.loop(1, 32)
    def _(d):
        pl.semaphore_signal(barrier, inc=1, device_id=((f + d) % 32, t), device_id_type=MESH)

    for peer in [tdev(1 - zh, y)] + [tdev(zh, (y + d) % 4) for d in FAR]:
        pl.semaphore_signal(barrier, inc=1, device_id=peer, device_id_type=MESH)

    def core_copy(s, dx, z):
        return remote(
            cs.at[s, dx, z], cr.at[s, dx, z], c_s.at[s, dx, z], c_r.at[s, dx, z], fdev(x, zl, 1 - c)
        )

    def relay_copy(s, i):
        return remote(
            xq.at[s, i], xqr.at[s, i], q_s.at[s, i], q_r.at[s, i], fdev((x + 1 + i // 2 * 2) % 4, zl, c)
        )

    def x_copy(s, way, i):
        return remote(
            xs.at[s, way, i], xr.at[s, way, i], x_s.at[s, way, i], x_r.at[s, way, i],
            fdev((x + 1 + 2 * way) % 4, zl, c),
        )

    def z_copy(s, dz):
        return remote(
            zs.at[s, dz - 1], zr.at[s, dz - 1], z_s.at[s, dz - 1], z_r.at[s, dz - 1],
            fdev(x, (zl + dz) % 4, c),
        )

    def tp_copies(view, ss, rs):
        own = view(t)
        other = view((1 - zh) * 4 + y)
        first = [remote(own, own, ss(0), rs(0), tdev(1 - zh, y))]
        first += [remote(own, own, ss(d), rs(d), tdev(zh, (y + d) % 4)) for d in FAR]
        second = [remote(other, other, ss(3 + d), rs(3 + d), tdev(zh, (y + d) % 4)) for d in FAR]
        return first, second

    left_first, left_second = tp_copies(lambda k: lm.at[k], lambda i: l_s.at[i], lambda i: l_r.at[i])
    g_copies = [
        tp_copies(lambda k, s=s: ag.at[s, k], lambda i, s=s: g_s.at[s, i], lambda i, s=s: g_r.at[s, i])
        for s in range(2)
    ]
    h_copies = [
        [
            remote(ah.at[s, t], ah.at[s, t], h_s.at[s, d - 1], h_r.at[s, d - 1], tdev(zh, (y + d) % 4))
            for d in FAR
        ]
        for s in range(2)
    ]
    p_copies = [remote(pb.at[s], pbr.at[s], p_s.at[s], p_r.at[s], tdev(1 - zh, y)) for s in range(2)]
    right_copies = [
        remote(rmsg.at[(y + d) % 4], rc.at[y], r_s.at[d - 1], r_r.at[d - 1], tdev(zh, (y + d) % 4)) for d in FAR
    ]

    def a2a_copy(d):
        k = (f + d) % 32
        return remote(a2s.at[k], a2r.at[f], a_s.at[d], a_r.at[d], (k, t))

    def start(copies):
        for cp in copies:
            cp.start()

    leaving = {}

    def left_device(*name):
        leaving.pop(name)()

    def wait_sent(copies):
        for cp in copies:
            cp.wait_send()

    pl.semaphore_wait(barrier, 35)

    def stacked(v):
        return jnp.concatenate([v[:, q * 128 : q * 128 + 128] for q in range(4)], axis=0)

    def send_left():
        loads[0].wait()
        for s in range(2):
            encode(stacked(bl[s]), lm.at[t, s])
        start(left_first)
        leaving["left", 0] = lambda: wait_sent(left_first)

    def send_right():
        loads[1].wait()
        lanes = lane_iota(64)
        for u in range(4):
            a = br[0, :, u * 128 : u * 128 + 128]
            b = br[1, :, u * 128 : u * 128 + 128]
            even, odd = jnp.where(lanes < 64, a, roll_half(b)), jnp.where(lanes < 64, roll_half(a), b)
            for k, v in ((2 * u, even), (2 * u + 1, odd)):
                high, low = split(v)
                rmsg[k % 4, k // 4, 0] = high
                rmsg[k % 4, k // 4, 1] = low
        rc[y] = rmsg[y]
        start(right_copies)
        leaving["right", 0] = lambda: wait_sent(right_copies)

    def extract(slot):
        b = bos[slot]
        half = b % 2
        first = ((b % 16) // 2 * 4 + b // 16) * 2
        near = g[first + half]
        away = g[first + 1 - half]
        upper = (lane_iota(256) >= 64).astype(i32)
        return jnp.where(upper == half, near, roll_half(away))

    def slot_of(s, dx, z, core):
        return ((((x + dx) % 4) * 4 + z) * 2 + core) * 2 + s

    def core_part(s, dx):
        @pl.loop(0, 4)
        def _(j):
            z = (zl + 1 + j // 2 + 2 * (j % 2)) % 4
            cs[s, dx, z] = extract(slot_of(s, dx, z, 1 - c))
            core_copy(s, dx, z).start()

        def sent():
            @pl.loop(0, 4)
            def _(z):
                core_copy(s, dx, z).wait_send()

        leaving["core", s, dx] = sent

    def pair_sum(s, dx, z):
        own = extract(slot_of(s, dx, z, c))
        core_copy(s, dx, z).wait_recv()
        return own + cr[s, dx, z]

    def relay_stage(s):
        @pl.loop(0, 4)
        def _(j):
            i = j // 2 + 2 * (j % 2)
            encode(pair_sum(s, 2, (zl + 1 + i) % 4), xq.at[s, i])
            relay_copy(s, i).start()

        def sent():
            @pl.loop(0, 4)
            def _(i):
                relay_copy(s, i).wait_send()

        leaving["relay", s] = sent

    def near_stage(s, j):
        for way in (1, 0):
            i = j + 2 - 2 * way
            encode(pair_sum(s, 1 + 2 * way, (zl + 1 + i) % 4), xs.at[s, way, i])
            x_copy(s, way, i).start()
        leaving["near", s, j] = lambda: wait_sent([x_copy(s, 1, j), x_copy(s, 0, j + 2)])

    def relayed_stage(s, j):
        for way in (0, 1):
            i = j + 2 * way
            own = pair_sum(s, 1 + 2 * way, (zl + 1 + i) % 4)
            relay_copy(s, i).wait_recv()
            encode(own + decode(xqr.at[s, i]), xs.at[s, way, i])
            x_copy(s, way, i).start()
        leaving["relayed", s, j] = lambda: wait_sent([x_copy(s, 0, j), x_copy(s, 1, j + 2)])

    def x_sum(s, i):
        total = pair_sum(s, 0, (zl + 1 + i) % 4)
        for way in range(2):
            x_copy(s, way, i).wait_recv()
            total += decode(xr.at[s, way, i])
        return total

    def z_send(s, dz):
        encode(x_sum(s, dz - 1), zs.at[s, dz - 1])
        z_copy(s, dz).start()
        leaving["z", s, dz] = lambda: z_copy(s, dz).wait_send()

    def z_keep(s):
        za[s] = x_sum(s, 3)

    def g_stage(s):
        total = za[s]
        for dz in range(1, 4):
            z_copy(s, dz).wait_recv()
            total += decode(zr.at[s, dz - 1])
        turned = total.T
        a, b = turned[0:64], turned[64:128]
        gslab[s, :, 0:256] = a
        gslab[s, :, 256:512] = b
        encode(jnp.concatenate([a[:, :128], a[:, 128:], b[:, :128], b[:, 128:]], axis=0), ag.at[s, t])
        start(g_copies[s][0])
        leaving["g", s] = lambda: wait_sent(g_copies[s][0])

    def forward(name, s, copies):
        copies[0][0].wait_recv()
        start(copies[1])
        leaving["forward", name, s] = lambda: wait_sent(copies[1])

    def unpack(message, s, store, half):
        @pl.loop(0, 4)
        def _(j):
            k = half * 4 + j
            v = decode(message(k))
            rows = pl.ds(pl.multiple_of(k * 64, 64), 64)
            for q in range(4):
                high, low = split(v[q * 64 : q * 64 + 64])
                store[s, 0, rows, q * 128 : q * 128 + 128] = high
                store[s, 1, rows, q * 128 : q * 128 + 128] = low

    def half_product(a, store, s, half):
        k = pl.ds(pl.multiple_of(half * 256, 256), 256)
        return dot3(a(k), store[s, 0, k, :], store[s, 1, k, :], PLAIN)

    def near_half(copies, messages, s, store, a):
        for cp in copies:
            cp.wait_recv()
        unpack(lambda k: messages.at[s, k], s, store, zh)
        return half_product(a, store, s, zh)

    def far_half(copies, messages, s, store, a):
        for cp in copies:
            cp.wait_recv()
        unpack(lambda k: messages.at[s, k], s, store, 1 - zh)
        return half_product(a, store, s, 1 - zh)

    def put(ref, dst, i, s):
        return pltpu.make_async_copy(ref.at[s], dst.at[s], out_sem.at[i, s])

    def rotate_near(s):
        part[s] = near_half(g_copies[s][0][1:], ag, s, gt, lambda k: br[s, :, k])

    def rotate(s):
        partial = part[s] + far_half(g_copies[s][1], ag, s, gt, lambda k: br[s, :, k])
        rotated = dot3(partial, left[s, 0], left[s, 1], MINOR)
        new_moment = first_decay * mo[s] + (1.0 - first_decay) * rotated
        new_second = second_decay * se[s] + (1.0 - second_decay) * rotated * rotated
        mo[s] = new_moment
        se[s] = new_second
        direction = new_moment / (jnp.sqrt(new_second) + epsilon)
        half = dot3(direction, left[s, 0], left[s, 1], PLAIN)
        encode(stacked(half), ah.at[s, t])
        start(h_copies[s])
        leaving["h", s] = lambda: wait_sent(h_copies[s])
        put(mo, nm, 0, s).start()
        put(se, ns, 1, s).start()

    def statistics(s):
        right = dot3(gslab[s], gt[s, 0], gt[s, 1], MINOR)
        sr[s] = second_decay * sr[s] + (1.0 - second_decay) * right
        put(sr, nr, 2, s).start()
        cols = pl.ds(pl.multiple_of((t // 2) * 128, 128), 128)
        rows = gt[s, 0, :, cols].astype(f32) + gt[s, 1, :, cols].astype(f32)
        tmp[...] = rows.T
        mine = tmp[pl.ds(pl.multiple_of((t % 2) * 64, 64), 64), :]
        out = dot3(mine, gt[s, 0], gt[s, 1], PLAIN)
        sl[s] = second_decay * sl[s] + (1.0 - second_decay) * out
        put(sl, nl, 3, s).start()

    def back_near(s):
        rows = pl.ds(s * 64, 64)
        both = near_half(
            h_copies[s], ah, s, hb, lambda k: jnp.concatenate([rct[1 - zh, rows, :], rct[zh, rows, :]], axis=0)
        )
        encode(stacked(both[0:64]), pb.at[s])
        p_copies[s].start()
        leaving["p", s] = lambda: p_copies[s].wait_send()
        bk[rows, :] = both[64:128]

    def back(s):
        p_copies[s].wait_recv()
        other = decode(pbr.at[s])
        for q in range(4):
            bk[s * 64 : s * 64 + 64, q * 128 : q * 128 + 128] += other[q * 64 : q * 64 + 64]

    def grad_ready():
        @pl.loop(0, 8)
        def _(i):
            grad_load(i).wait()

    def right_ready():
        for cp in right_copies:
            cp.wait_recv()
        for h in range(2):
            rct[h] = jnp.concatenate([rc[k, h, 0].astype(f32) + rc[k, h, 1].astype(f32) for k in range(4)], axis=0).T

    def left_ready():
        for cp in loads[2:]:
            cp.wait()
        for cp in left_first[1:] + left_second:
            cp.wait_recv()
        for s in range(2):
            unpack(lambda k: lm.at[k, s], s, left, 0)
            unpack(lambda k: lm.at[k, s], s, left, 1)

    def send_back():
        rows = bk[...].T.astype(bf16)
        for k in range(32):
            a2s[k] = rows[k * 16 : k * 16 + 16]

        @pl.loop(0, 31)
        def _(d):
            a2a_copy((d + 15) % 31 + 1).start()

        a2r[f] = a2s[f]

    steps = [
        lambda: grad_ready(),
        lambda: core_part(0, 2),
        lambda: core_part(0, 3),
        lambda: core_part(0, 1),
        lambda: send_left(),
        lambda: relay_stage(0),
        lambda: send_right(),
        lambda: core_part(0, 0),
        lambda: core_part(1, 2),
        lambda: near_stage(0, 0),
        lambda: near_stage(0, 1),
        lambda: core_part(1, 3),
        lambda: relayed_stage(0, 0),
        lambda: relayed_stage(0, 1),
        lambda: core_part(1, 1),
        lambda: left_device("near", 0, 0),
        lambda: left_device("near", 0, 1),
        lambda: relay_stage(1),
        lambda: core_part(1, 0),
        lambda: z_send(0, 1),
        lambda: z_send(0, 3),
        lambda: z_send(0, 2),
        lambda: z_keep(0),
        lambda: near_stage(1, 0),
        lambda: near_stage(1, 1),
        lambda: relayed_stage(1, 0),
        lambda: relayed_stage(1, 1),
        lambda: forward("left", 0, (left_first, left_second)),
        lambda: g_stage(0),
        lambda: z_send(1, 1),
        lambda: z_send(1, 3),
        lambda: z_send(1, 2),
        lambda: z_keep(1),
        lambda: left_ready(),
        lambda: forward("g", 0, g_copies[0]),
        lambda: rotate_near(0),
        lambda: g_stage(1),
        lambda: rotate(0),
        lambda: forward("g", 1, g_copies[1]),
        lambda: rotate_near(1),
        lambda: right_ready(),
        lambda: back_near(0),
        lambda: rotate(1),
        lambda: statistics(0),
        lambda: back_near(1),
        lambda: back(0),
        lambda: statistics(1),
        lambda: back(1),
        lambda: send_back(),
    ]
    for step in steps:
        step()

    for sent in list(leaving.values()):
        sent()
    for s in range(2):
        for i, (ref, dst) in enumerate(((mo, nm), (se, ns), (sr, nr), (sl, nl))):
            put(ref, dst, i, s).wait()

    @pl.loop(1, 32)
    def _(d):
        a2a_copy(d).wait()


def finish(bos, rows, nl, nr, nm, ns, upd_out, nl_out, nr_out, nm_out, ns_out, upd, sem):
    outs = [
        pltpu.make_async_copy(src, dst, sem.at[i])
        for i, (src, dst) in enumerate(((nl, nl_out), (nr, nr_out), (nm, nm_out), (ns, ns_out), (upd, upd_out)))
    ]
    for out in outs[:4]:
        out.start()

    upper = lane_iota(16) >= 64

    for k in range(32):
        both = rows[k].astype(f32)
        turned = roll_half(both)
        for j in range(2):
            b = bos[2 * k + j]
            half = b & 1
            cols = pl.ds(pl.multiple_of(((b & 15) >> 1) * 128, 128), 128)
            old = upd[b >> 4, :, cols]
            new = jnp.where((lane_iota(16) * 0 + half) == j, both, turned).astype(bf16)
            upd[b >> 4, :, cols] = jnp.where(upper == ((lane_iota(16) * 0 + half) == 1), new, old)

    outs[4].start()
    for out in outs:
        out.wait()


def local(grad_part, block_of_slot, stat_left, stat_right, basis_left, basis_right, moment, second):
    smem = pl.BlockSpec(memory_space=pltpu.SMEM)
    hbm = pl.BlockSpec(memory_space=pl.ANY)
    state = jax.ShapeDtypeStruct((2, 64, 512), f32)
    vmem = pl.BlockSpec(memory_space=pltpu.VMEM)
    v = pltpu.VMEM
    dma = pltpu.SemaphoreType.DMA
    outs = pl.pallas_call(
        kernel,
        name="step",
        out_shape=(jax.ShapeDtypeStruct((32, 16, 128), bf16), state, state, state, state),
        in_specs=[smem] + [hbm] * 7,
        out_specs=(vmem, hbm, hbm, hbm, hbm),
        scratch_shapes=[
            v((64, 256, 128), f32),
            *[v((2, 64, 512), f32)] * 6,
            v((2, 4, 4, 256, 128), f32),
            v((2, 4, 4, 256, 128), f32),
            v((2, 4, 272, 128), i16),
            v((2, 4, 272, 128), i16),
            v((2, 2, 4, 272, 128), i16),
            v((2, 2, 4, 272, 128), i16),
            v((2, 3, 272, 128), i16),
            v((2, 3, 272, 128), i16),
            v((2, 256, 128), f32),
            v((2, 64, 512), f32),
            v((2, 8, 272, 128), i16),
            v((2, 8, 272, 128), i16),
            v((8, 2, 272, 128), i16),
            v((2, 2, 512, 512), bf16),
            v((4, 2, 2, 64, 128), bf16),
            v((4, 2, 2, 64, 128), bf16),
            v((2, 128, 256), f32),
            v((2, 2, 512, 512), bf16),
            v((2, 2, 512, 512), bf16),
            v((128, 512), f32),
            v((128, 512), f32),
            v((2, 64, 512), f32),
            v((2, 272, 128), i16),
            v((2, 272, 128), i16),
            v((32, 16, 128), bf16),
            dma((6,)),
            dma((8,)),
            dma((4, 2)),
            *[dma((2, 4, 4))] * 2,
            *[dma((2, 4))] * 2,
            *[dma((2, 2, 4))] * 2,
            *[dma((2, 3))] * 2,
            *[dma((7,))] * 2,
            *[dma((3,))] * 2,
            *[dma((2, 7))] * 2,
            *[dma((2, 3))] * 2,
            *[dma((2,))] * 2,
            *[dma((32,))] * 2,
        ],
        compiler_params=pltpu.CompilerParams(
            collective_id=0, has_side_effects=True, vmem_limit_bytes=vmem_bytes
        ),
    )(block_of_slot, grad_part.reshape(8, 256, 1024), stat_left, stat_right, basis_left, basis_right, moment, second)
    return pl.pallas_call(
        finish,
        name="finish",
        out_shape=(jax.ShapeDtypeStruct((4, 16, 1024), bf16), state, state, state, state),
        in_specs=[smem] + [vmem] * 5,
        out_specs=(hbm,) * 5,
        scratch_shapes=[v((4, 16, 1024), bf16), dma((5,))],
        compiler_params=pltpu.CompilerParams(vmem_limit_bytes=vmem_bytes),
    )(block_of_slot, *outs)


def solution(mesh):
    return jax.shard_map(
        local,
        mesh=mesh,
        in_specs=(
            P("fsdp", None, None, "tp"),
            P(),
            P("fsdp", "tp", None),
            P("fsdp", "tp", None),
            P("fsdp", "tp", None),
            P("fsdp", "tp", None),
            P("fsdp", "tp", None),
            P("fsdp", "tp", None),
        ),
        out_specs=(
            P(None, "fsdp", "tp"),
            P("fsdp", "tp", None),
            P("fsdp", "tp", None),
            P("fsdp", "tp", None),
            P("fsdp", "tp", None),
        ),
        check_vma=False,
    )
```

```python
import jax
import jax.numpy as jnp
from jax import lax
from jax.experimental import pallas as pl
from jax.experimental.pallas import tpu as pltpu
from jax.sharding import PartitionSpec as P

first_decay = 0.9
second_decay = 0.95
epsilon = 1e-08
MESH = pl.DeviceIdType.MESH
f32, bf16, i16, i32 = jnp.float32, jnp.bfloat16, jnp.int16, jnp.int32
FAR = (2, 1, 3)
vmem_bytes = 64 * 2**20 - 19 * 2**16


def roll_half(v):
    return pltpu.roll(v, 64, 1)


def lane_iota(rows):
    return lax.broadcasted_iota(i32, (rows, 128), 1)


def split(v):
    high = v.astype(bf16)
    return high, (v - high.astype(f32)).astype(bf16)


def dot(a, b, dims):
    return lax.dot_general(a, b, (dims, ((), ())), preferred_element_type=f32)


PLAIN = ((1,), (0,))
MINOR = ((1,), (1,))


def dot3(a, bh, bl, dims):
    ah, al = split(a)
    n = a.shape[0]
    both = dot(jnp.concatenate([ah, al], axis=0), bh, dims)
    return both[:n] + (dot(ah, bl, dims) + both[n:])


def encode(v, ref):
    top = jnp.max(jnp.abs(v), axis=0, keepdims=True)
    power = jnp.ceil(jnp.log2(jnp.maximum(top, 1e-30) * (1.0 / 32500.0)))
    ref[pl.ds(0, 256), :] = jnp.round(v * jnp.exp2(-power)).astype(i32).astype(i16)
    ref[pl.ds(256, 16), :] = jnp.broadcast_to(power, (16, 128)).astype(i32).astype(i16)


def scale_of(ref):
    return jnp.exp2(ref[pl.ds(256, 16), :].astype(i32).astype(f32))[0:1]


def decode(ref):
    return ref[pl.ds(0, 256), :].astype(i32).astype(f32) * scale_of(ref)


def kernel(
    bos, grad_h, sl_h, sr_h, bl_h, br_h, mo_h, se_h,
    a2r, nl, nr, nm, ns,
    g, sl, sr, bl, br, mo, se,
    cs, cr, xq, xqr, xs, xr, zs, zr, za, gslab, ag, ah, lm, left, left_t, rmsg, rc, rct, gt, hb, tmp, bk, part, pb, pbr, a2s,
    loc, g_sem, out_sem, c_s, c_r, q_s, q_r, x_s, x_r, z_s, z_r, l_s, l_r, r_s, r_r, g_s, g_r, h_s, h_r, p_s, p_r, a_s, a_r,
):
    f = lax.axis_index("fsdp")
    t = lax.axis_index("tp")
    x, zl, c = f // 8, (f // 2) % 4, f % 2
    zh, y = t // 4, t % 4

    def fdev(x_, z_, c_):
        return ((x_ * 4 + z_) * 2 + c_, t)

    def tdev(zh_, y_):
        return (f, zh_ * 4 + y_)

    def remote(src, dst, ss, rs, dev):
        return pltpu.make_async_remote_copy(
            src_ref=src, dst_ref=dst, send_sem=ss, recv_sem=rs, device_id=dev, device_id_type=MESH
        )

    loads = [
        pltpu.make_async_copy(src, dst, loc.at[i])
        for i, (src, dst) in enumerate(((bl_h, bl), (br_h, br), (sl_h, sl), (sr_h, sr), (mo_h, mo), (se_h, se)))
    ]

    def grad_load(i):
        return pltpu.make_async_copy(
            grad_h.at[:, :, pl.ds(pl.multiple_of(i * 128, 128), 128)], g.at[pl.ds(8 * i, 8)], g_sem.at[i]
        )

    @pl.loop(0, 8)
    def _(i):
        grad_load(i).start()

    for cp in loads:
        cp.start()

    barrier = pltpu.get_barrier_semaphore()

    @pl.loop(1, 32)
    def _(d):
        pl.semaphore_signal(barrier, inc=1, device_id=((f + d) % 32, t), device_id_type=MESH)

    for peer in [tdev(1 - zh, y)] + [tdev(zh, (y + d) % 4) for d in FAR]:
        pl.semaphore_signal(barrier, inc=1, device_id=peer, device_id_type=MESH)

    def core_copy(s, dx, z):
        return remote(
            cs.at[s, dx, z], cr.at[s, dx, z], c_s.at[s, dx, z], c_r.at[s, dx, z], fdev(x, zl, 1 - c)
        )

    def relay_copy(s, i):
        return remote(
            xq.at[s, i], xqr.at[s, i], q_s.at[s, i], q_r.at[s, i], fdev((x + 1 + i // 2 * 2) % 4, zl, c)
        )

    def x_copy(s, way, i):
        return remote(
            xs.at[s, way, i], xr.at[s, way, i], x_s.at[s, way, i], x_r.at[s, way, i],
            fdev((x + 1 + 2 * way) % 4, zl, c),
        )

    def z_copy(s, dz):
        return remote(
            zs.at[s, dz - 1], zr.at[s, dz - 1], z_s.at[s, dz - 1], z_r.at[s, dz - 1],
            fdev(x, (zl + dz) % 4, c),
        )

    def tp_copies(view, ss, rs):
        own = view(t)
        other = view((1 - zh) * 4 + y)
        first = [remote(own, own, ss(0), rs(0), tdev(1 - zh, y))]
        first += [remote(own, own, ss(d), rs(d), tdev(zh, (y + d) % 4)) for d in FAR]
        second = [remote(other, other, ss(3 + d), rs(3 + d), tdev(zh, (y + d) % 4)) for d in FAR]
        return first, second

    left_first, left_second = tp_copies(lambda k: lm.at[k], lambda i: l_s.at[i], lambda i: l_r.at[i])
    g_copies = [
        tp_copies(lambda k, s=s: ag.at[s, k], lambda i, s=s: g_s.at[s, i], lambda i, s=s: g_r.at[s, i])
        for s in range(2)
    ]
    h_copies = [
        [
            remote(ah.at[s, t], ah.at[s, t], h_s.at[s, d - 1], h_r.at[s, d - 1], tdev(zh, (y + d) % 4))
            for d in FAR
        ]
        for s in range(2)
    ]
    p_copies = [remote(pb.at[s], pbr.at[s], p_s.at[s], p_r.at[s], tdev(1 - zh, y)) for s in range(2)]
    right_copies = [
        remote(rmsg.at[(y + d) % 4], rc.at[y], r_s.at[d - 1], r_r.at[d - 1], tdev(zh, (y + d) % 4)) for d in FAR
    ]

    def a2a_copy(d):
        k = (f + d) % 32
        return remote(a2s.at[k], a2r.at[f], a_s.at[d], a_r.at[d], (k, t))

    def start(copies):
        for cp in copies:
            cp.start()

    leaving = {}

    def left_device(*name):
        leaving.pop(name)()

    def wait_sent(copies):
        for cp in copies:
            cp.wait_send()

    pl.semaphore_wait(barrier, 35)

    def stacked(v):
        return jnp.concatenate([v[:, q * 128 : q * 128 + 128] for q in range(4)], axis=0)

    def send_left():
        loads[0].wait()
        for s in range(2):
            encode(stacked(bl[s]), lm.at[t, s])
        start(left_first)
        leaving["left", 0] = lambda: wait_sent(left_first)

    def send_right():
        loads[1].wait()
        lanes = lane_iota(64)
        for u in range(4):
            a = br[0, :, u * 128 : u * 128 + 128]
            b = br[1, :, u * 128 : u * 128 + 128]
            even, odd = jnp.where(lanes < 64, a, roll_half(b)), jnp.where(lanes < 64, roll_half(a), b)
            for k, v in ((2 * u, even), (2 * u + 1, odd)):
                high, low = split(v)
                rmsg[k % 4, k // 4, 0] = high
                rmsg[k % 4, k // 4, 1] = low
        rc[y] = rmsg[y]
        start(right_copies)
        leaving["right", 0] = lambda: wait_sent(right_copies)

    def extract(slot):
        b = bos[slot]
        half = b % 2
        first = ((b % 16) // 2 * 4 + b // 16) * 2
        near = g[first + half]
        away = g[first + 1 - half]
        upper = (lane_iota(256) >= 64).astype(i32)
        return jnp.where(upper == half, near, roll_half(away))

    def slot_of(s, dx, z, core):
        return ((((x + dx) % 4) * 4 + z) * 2 + core) * 2 + s

    def core_part(s, dx):
        @pl.loop(0, 4)
        def _(j):
            z = (zl + 1 + j // 2 + 2 * (j % 2)) % 4
            cs[s, dx, z] = extract(slot_of(s, dx, z, 1 - c))
            core_copy(s, dx, z).start()

        def sent():
            @pl.loop(0, 4)
            def _(z):
                core_copy(s, dx, z).wait_send()

        leaving["core", s, dx] = sent

    def pair_sum(s, dx, z):
        own = extract(slot_of(s, dx, z, c))
        core_copy(s, dx, z).wait_recv()
        return own + cr[s, dx, z]

    def relay_stage(s):
        @pl.loop(0, 4)
        def _(j):
            i = j // 2 + 2 * (j % 2)
            encode(pair_sum(s, 2, (zl + 1 + i) % 4), xq.at[s, i])
            relay_copy(s, i).start()

        def sent():
            @pl.loop(0, 4)
            def _(i):
                relay_copy(s, i).wait_send()

        leaving["relay", s] = sent

    def near_stage(s, j):
        for way in (1, 0):
            i = j + 2 - 2 * way
            encode(pair_sum(s, 1 + 2 * way, (zl + 1 + i) % 4), xs.at[s, way, i])
            x_copy(s, way, i).start()
        leaving["near", s, j] = lambda: wait_sent([x_copy(s, 1, j), x_copy(s, 0, j + 2)])

    def relayed_stage(s, j):
        for way in (0, 1):
            i = j + 2 * way
            own = pair_sum(s, 1 + 2 * way, (zl + 1 + i) % 4)
            relay_copy(s, i).wait_recv()
            encode(own + decode(xqr.at[s, i]), xs.at[s, way, i])
            x_copy(s, way, i).start()
        leaving["relayed", s, j] = lambda: wait_sent([x_copy(s, 0, j), x_copy(s, 1, j + 2)])

    def x_sum(s, i):
        total = pair_sum(s, 0, (zl + 1 + i) % 4)
        for way in range(2):
            x_copy(s, way, i).wait_recv()
            total += decode(xr.at[s, way, i])
        return total

    def z_send(s, dz):
        encode(x_sum(s, dz - 1), zs.at[s, dz - 1])
        z_copy(s, dz).start()
        leaving["z", s, dz] = lambda: z_copy(s, dz).wait_send()

    def z_keep(s):
        za[s] = x_sum(s, 3)

    def g_stage(s):
        total = za[s]
        for dz in range(1, 4):
            z_copy(s, dz).wait_recv()
            total += decode(zr.at[s, dz - 1])
        turned = total.T
        a, b = turned[0:64], turned[64:128]
        gslab[s, :, 0:256] = a
        gslab[s, :, 256:512] = b
        encode(jnp.concatenate([a[:, :128], a[:, 128:], b[:, :128], b[:, 128:]], axis=0), ag.at[s, t])
        start(g_copies[s][0])
        leaving["g", s] = lambda: wait_sent(g_copies[s][0])

    def forward(name, s, copies):
        copies[0][0].wait_recv()
        start(copies[1])
        leaving["forward", name, s] = lambda: wait_sent(copies[1])

    def unpack(message, s, store, half):
        @pl.loop(0, 4)
        def _(j):
            k = half * 4 + j
            v = decode(message(k))
            rows = pl.ds(pl.multiple_of(k * 64, 64), 64)
            for q in range(4):
                high, low = split(v[q * 64 : q * 64 + 64])
                store[s, 0, rows, q * 128 : q * 128 + 128] = high
                store[s, 1, rows, q * 128 : q * 128 + 128] = low

    def half_product(a, store, s, half):
        k = pl.ds(pl.multiple_of(half * 256, 256), 256)
        return dot3(a(k), store[s, 0, k, :], store[s, 1, k, :], PLAIN)

    def near_half(copies, messages, s, store, a):
        for cp in copies:
            cp.wait_recv()
        unpack(lambda k: messages.at[s, k], s, store, zh)
        return half_product(a, store, s, zh)

    def far_half(copies, messages, s, store, a):
        for cp in copies:
            cp.wait_recv()
        unpack(lambda k: messages.at[s, k], s, store, 1 - zh)
        return half_product(a, store, s, 1 - zh)

    def put(ref, dst, i, s):
        return pltpu.make_async_copy(ref.at[s], dst.at[s], out_sem.at[i, s])

    def rotate_near(s):
        part[s] = near_half(g_copies[s][0][1:], ag, s, gt, lambda k: br[s, :, k])

    def rotate(s):
        partial = part[s] + far_half(g_copies[s][1], ag, s, gt, lambda k: br[s, :, k])
        rotated = dot3(partial, left_t[s, 0], left_t[s, 1], PLAIN)
        new_moment = first_decay * mo[s] + (1.0 - first_decay) * rotated
        new_second = second_decay * se[s] + (1.0 - second_decay) * rotated * rotated
        mo[s] = new_moment
        se[s] = new_second
        direction = new_moment / (jnp.sqrt(new_second) + epsilon)
        half = dot3(direction, left[s, 0], left[s, 1], PLAIN)
        encode(stacked(half), ah.at[s, t])
        start(h_copies[s])
        leaving["h", s] = lambda: wait_sent(h_copies[s])
        put(mo, nm, 0, s).start()
        put(se, ns, 1, s).start()

    def statistics(s):
        right = dot3(gslab[s], gt[s, 0], gt[s, 1], MINOR)
        sr[s] = second_decay * sr[s] + (1.0 - second_decay) * right
        put(sr, nr, 2, s).start()
        cols = pl.ds(pl.multiple_of((t // 2) * 128, 128), 128)
        rows = gt[s, 0, :, cols].astype(f32) + gt[s, 1, :, cols].astype(f32)
        tmp[...] = rows.T
        mine = tmp[pl.ds(pl.multiple_of((t % 2) * 64, 64), 64), :]
        out = dot3(mine, gt[s, 0], gt[s, 1], PLAIN)
        sl[s] = second_decay * sl[s] + (1.0 - second_decay) * out
        put(sl, nl, 3, s).start()

    def back_near(s):
        rows = pl.ds(s * 64, 64)
        both = near_half(
            h_copies[s], ah, s, hb, lambda k: jnp.concatenate([rct[1 - zh, rows, :], rct[zh, rows, :]], axis=0)
        )
        encode(stacked(both[0:64]), pb.at[s])
        p_copies[s].start()
        leaving["p", s] = lambda: p_copies[s].wait_send()
        bk[rows, :] = both[64:128]

    def back(s):
        p_copies[s].wait_recv()
        other = decode(pbr.at[s])
        for q in range(4):
            bk[s * 64 : s * 64 + 64, q * 128 : q * 128 + 128] += other[q * 64 : q * 64 + 64]

    def grad_ready():
        @pl.loop(0, 8)
        def _(i):
            grad_load(i).wait()

    def right_ready():
        for cp in right_copies:
            cp.wait_recv()
        for h in range(2):
            rct[h] = jnp.concatenate([rc[k, h, 0].astype(f32) + rc[k, h, 1].astype(f32) for k in range(4)], axis=0).T

    def left_ready():
        for cp in loads[2:]:
            cp.wait()
        for cp in left_first[1:] + left_second:
            cp.wait_recv()
        for s in range(2):
            unpack(lambda k: lm.at[k, s], s, left, 0)
            unpack(lambda k: lm.at[k, s], s, left, 1)
            for h in range(2):
                left_t[s, h] = left[s, h].T

    def send_back():
        rows = bk[...].T.astype(bf16)
        for k in range(32):
            a2s[k] = rows[k * 16 : k * 16 + 16]

        @pl.loop(0, 31)
        def _(d):
            a2a_copy((d + 15) % 31 + 1).start()

        a2r[f] = a2s[f]

    steps = [
        lambda: grad_ready(),
        lambda: core_part(0, 2),
        lambda: core_part(0, 3),
        lambda: core_part(0, 1),
        lambda: send_left(),
        lambda: relay_stage(0),
        lambda: send_right(),
        lambda: core_part(0, 0),
        lambda: core_part(1, 2),
        lambda: near_stage(0, 0),
        lambda: near_stage(0, 1),
        lambda: core_part(1, 3),
        lambda: relayed_stage(0, 0),
        lambda: relayed_stage(0, 1),
        lambda: core_part(1, 1),
        lambda: left_device("near", 0, 0),
        lambda: left_device("near", 0, 1),
        lambda: relay_stage(1),
        lambda: core_part(1, 0),
        lambda: z_send(0, 1),
        lambda: z_send(0, 3),
        lambda: z_send(0, 2),
        lambda: z_keep(0),
        lambda: near_stage(1, 0),
        lambda: near_stage(1, 1),
        lambda: relayed_stage(1, 0),
        lambda: relayed_stage(1, 1),
        lambda: forward("left", 0, (left_first, left_second)),
        lambda: g_stage(0),
        lambda: z_send(1, 1),
        lambda: z_send(1, 3),
        lambda: z_send(1, 2),
        lambda: z_keep(1),
        lambda: left_ready(),
        lambda: forward("g", 0, g_copies[0]),
        lambda: rotate_near(0),
        lambda: g_stage(1),
        lambda: rotate(0),
        lambda: forward("g", 1, g_copies[1]),
        lambda: rotate_near(1),
        lambda: right_ready(),
        lambda: back_near(0),
        lambda: rotate(1),
        lambda: statistics(0),
        lambda: back_near(1),
        lambda: back(0),
        lambda: statistics(1),
        lambda: back(1),
        lambda: send_back(),
    ]
    for step in steps:
        step()

    for sent in list(leaving.values()):
        sent()
    for s in range(2):
        for i, (ref, dst) in enumerate(((mo, nm), (se, ns), (sr, nr), (sl, nl))):
            put(ref, dst, i, s).wait()

    @pl.loop(1, 32)
    def _(d):
        a2a_copy(d).wait()


def finish(bos, rows, nl, nr, nm, ns, upd_out, nl_out, nr_out, nm_out, ns_out, upd, sem):
    outs = [
        pltpu.make_async_copy(src, dst, sem.at[i])
        for i, (src, dst) in enumerate(((nl, nl_out), (nr, nr_out), (nm, nm_out), (ns, ns_out), (upd, upd_out)))
    ]
    for out in outs[:4]:
        out.start()

    upper = lane_iota(16) >= 64

    for k in range(32):
        both = rows[k].astype(f32)
        turned = roll_half(both)
        for j in range(2):
            b = bos[2 * k + j]
            half = b & 1
            cols = pl.ds(pl.multiple_of(((b & 15) >> 1) * 128, 128), 128)
            old = upd[b >> 4, :, cols]
            new = jnp.where((lane_iota(16) * 0 + half) == j, both, turned).astype(bf16)
            upd[b >> 4, :, cols] = jnp.where(upper == ((lane_iota(16) * 0 + half) == 1), new, old)

    outs[4].start()
    for out in outs:
        out.wait()


def local(grad_part, block_of_slot, stat_left, stat_right, basis_left, basis_right, moment, second):
    smem = pl.BlockSpec(memory_space=pltpu.SMEM)
    hbm = pl.BlockSpec(memory_space=pl.ANY)
    state = jax.ShapeDtypeStruct((2, 64, 512), f32)
    vmem = pl.BlockSpec(memory_space=pltpu.VMEM)
    v = pltpu.VMEM
    dma = pltpu.SemaphoreType.DMA
    outs = pl.pallas_call(
        kernel,
        name="step",
        out_shape=(jax.ShapeDtypeStruct((32, 16, 128), bf16), state, state, state, state),
        in_specs=[smem] + [hbm] * 7,
        out_specs=(vmem, hbm, hbm, hbm, hbm),
        scratch_shapes=[
            v((64, 256, 128), f32),
            *[v((2, 64, 512), f32)] * 6,
            v((2, 4, 4, 256, 128), f32),
            v((2, 4, 4, 256, 128), f32),
            v((2, 4, 272, 128), i16),
            v((2, 4, 272, 128), i16),
            v((2, 2, 4, 272, 128), i16),
            v((2, 2, 4, 272, 128), i16),
            v((2, 3, 272, 128), i16),
            v((2, 3, 272, 128), i16),
            v((2, 256, 128), f32),
            v((2, 64, 512), f32),
            v((2, 8, 272, 128), i16),
            v((2, 8, 272, 128), i16),
            v((8, 2, 272, 128), i16),
            v((2, 2, 512, 512), bf16),
            v((2, 2, 512, 512), bf16),
            v((4, 2, 2, 64, 128), bf16),
            v((4, 2, 2, 64, 128), bf16),
            v((2, 128, 256), f32),
            v((2, 2, 512, 512), bf16),
            v((2, 2, 512, 512), bf16),
            v((128, 512), f32),
            v((128, 512), f32),
            v((2, 64, 512), f32),
            v((2, 272, 128), i16),
            v((2, 272, 128), i16),
            v((32, 16, 128), bf16),
            dma((6,)),
            dma((8,)),
            dma((4, 2)),
            *[dma((2, 4, 4))] * 2,
            *[dma((2, 4))] * 2,
            *[dma((2, 2, 4))] * 2,
            *[dma((2, 3))] * 2,
            *[dma((7,))] * 2,
            *[dma((3,))] * 2,
            *[dma((2, 7))] * 2,
            *[dma((2, 3))] * 2,
            *[dma((2,))] * 2,
            *[dma((32,))] * 2,
        ],
        compiler_params=pltpu.CompilerParams(
            collective_id=0, has_side_effects=True, vmem_limit_bytes=vmem_bytes
        ),
    )(block_of_slot, grad_part.reshape(8, 256, 1024), stat_left, stat_right, basis_left, basis_right, moment, second)
    return pl.pallas_call(
        finish,
        name="finish",
        out_shape=(jax.ShapeDtypeStruct((4, 16, 1024), bf16), state, state, state, state),
        in_specs=[smem] + [vmem] * 5,
        out_specs=(hbm,) * 5,
        scratch_shapes=[v((4, 16, 1024), bf16), dma((5,))],
        compiler_params=pltpu.CompilerParams(vmem_limit_bytes=vmem_bytes),
    )(block_of_slot, *outs)


def solution(mesh):
    return jax.shard_map(
        local,
        mesh=mesh,
        in_specs=(
            P("fsdp", None, None, "tp"),
            P(),
            P("fsdp", "tp", None),
            P("fsdp", "tp", None),
            P("fsdp", "tp", None),
            P("fsdp", "tp", None),
            P("fsdp", "tp", None),
            P("fsdp", "tp", None),
        ),
        out_specs=(
            P(None, "fsdp", "tp"),
            P("fsdp", "tp", None),
            P("fsdp", "tp", None),
            P("fsdp", "tp", None),
            P("fsdp", "tp", None),
        ),
        check_vma=False,
    )
```
